128 devices in a mesh: row: 8 (over x, core), col: 16 (over z, y).
Axes of the slice: x: 4, y: 4, z: 4, core: 2. Of those that a mesh axis runs over, the one named last changes fastest.
Arguments:
- object_field: float32 [2, 8192, 4096], P(None, 'row', 'col'), may hold values from -5 to 5
- probe_modes: float32 [2, 3, 256, 256], replicated, may hold values from -6 to 6
- amplitudes: float32 [8, 16, 8, 256, 256], P('row', 'col'), may hold values from 0 to 3
- scan_offsets: int32 [8, 16, 8, 2], P('row', 'col'), may hold values from -128 to 8063, as said below
- slot_counts: int32 [8, 16], P('row', 'col'), may hold values from 1 to 8, as said below
Outputs:
- new_object: float32 [2, 8192, 4096], P(None, 'row', 'col')
- new_probe: float32 [2, 3, 256, 256], replicated
The draws below stay inside these ranges and needn't reach their ends.
Inputs may be any that keep to these rules, and one draw needn't show every extreme that they name: Each slot's window centre, scan_offsets + 128, lies in the tile of the device that holds the slot; slots at or past the tile's count carry offsets of the same kind but are not live. `slot_counts`: in every draw some tile has all 8 slots live and another has one.
All inputs are finite; a program needn't handle non-finite values.
Results may differ from the reference program's by a relative error of at most 0.0003.
Values sent between devices are 32-bit elements; how exact they have to be, the bound alone decides.
A program may use at most 128 MiB of HBM per device.

```python
import math
import jax
import jax.numpy as jnp
from jax import lax

PATCH = 256
MODES = 3
TILE_R = 1024
TILE_C = 256
CAP = 8
OBJ_R = 8192
OBJ_C = 4096
N_ROW = 8
N_COL = 16


def draw_scan_offsets(key, part):
    key = jax.random.fold_in(key, 11)
    row_key, col_key = jax.random.split(key)
    down = jax.random.randint(row_key, (N_ROW, N_COL, CAP), 0, TILE_R)
    across = jax.random.randint(col_key, (N_ROW, N_COL, CAP), 0, TILE_C)
    down = down.at[0, 0, 0].set(0)
    across = across.at[0, 0, 0].set(0)
    down = down.at[N_ROW - 1, N_COL - 1, 0].set(TILE_R - 1)
    across = across.at[N_ROW - 1, N_COL - 1, 0].set(TILE_C - 1)
    base_rows = (jnp.arange(N_ROW, dtype=jnp.int32) * TILE_R)[:, None, None]
    base_cols = (jnp.arange(N_COL, dtype=jnp.int32) * TILE_C)[None, :, None]
    tops = base_rows + down - PATCH // 2
    lefts = base_cols + across - PATCH // 2
    return jnp.stack([tops, lefts], axis=-1).astype(jnp.int32)


def draw_slot_counts(key, part):
    key = jax.random.fold_in(key, 23)
    first_key, second_key, third_key = jax.random.split(key, 3)
    tiles = N_ROW * N_COL
    values = jax.random.randint(first_key, (tiles,), 1, CAP + 1)
    fullest = jax.random.randint(second_key, (), 0, tiles)
    emptiest = (fullest + 1 + jax.random.randint(third_key, (), 0, tiles - 1)) % tiles
    places = jnp.arange(tiles, dtype=jnp.int32)
    values = jnp.where(places == fullest, CAP, values)
    values = jnp.where(places == emptiest, 1, values)
    return values.reshape(N_ROW, N_COL).astype(jnp.int32)


def levels(stream_key, extent, cuts, low, top_value):
    factor_of, own = 1.0, jax.random.fold_in(stream_key, 6)
    for position, blocks in cuts:
        draws = jnp.exp(jax.random.uniform(jax.random.fold_in(own, position), (blocks,), jnp.float32, low / len(cuts), top_value / len(cuts)))
        factor_of = factor_of * jnp.repeat(draws, extent[position] // blocks).reshape([-1 if axis == position else 1 for axis in range(len(extent))])
    return factor_of


def centred(own_key, shape, scale, reach, cuts=(), kind=jnp.bfloat16):
    entries = jax.random.normal(own_key, shape, jnp.float32) * scale
    if len(cuts) > 0:
        entries = levels(own_key, shape, cuts, -0.22, 0.18) * entries
    return jnp.clip(entries, min=-reach, max=reach).astype(kind)


def setup_inputs(seed: int = 0) -> dict:
    key_of = jax.random.split(jax.random.key(seed), 6)
    return {
        "object_field": centred(key_of[0], (2, OBJ_R, OBJ_C), 0.7, 5.0, ((1, 8), (2, 16)), jnp.float32),
        "probe_modes": centred(key_of[1], (2, MODES, PATCH, PATCH), 1.0, 6.0, (), jnp.float32),
        "amplitudes": jnp.clip(3.0 * jax.random.uniform(key_of[2], (N_ROW, N_COL, CAP, PATCH, PATCH), jnp.float32) ** levels(key_of[2], (N_ROW, N_COL, CAP, PATCH, PATCH), ((0, 8), (1, 16)), -0.2, 0.2), 0.0, 3.0),
        "scan_offsets": draw_scan_offsets(jax.random.fold_in(key_of[5], 71), 0),
        "slot_counts": draw_slot_counts(jax.random.fold_in(key_of[5], 71), 0),
    }


def reference(object_field, probe_modes, amplitudes, scan_offsets, slot_counts):
    half = PATCH // 2
    padded = jnp.pad(object_field, ((0, 0), (half, half), (half, half)))
    slots = N_ROW * N_COL * CAP
    offsets = scan_offsets.reshape(slots, 2).astype(jnp.int32)
    measured = amplitudes.reshape(slots, PATCH, PATCH)
    active = (jnp.arange(CAP, dtype=jnp.int32)[None, None, :] < slot_counts[:, :, None]).reshape(slots)
    active = active.astype(amplitudes.dtype)
    probe = probe_modes[0] + 1j * probe_modes[1]
    start_zero = jnp.zeros((), jnp.int32)

    def visit(carry, item):
        gradient, probe_grad = carry
        corner, target, weight = item
        top = (corner[0] + half).astype(jnp.int32)
        left = (corner[1] + half).astype(jnp.int32)
        window = lax.dynamic_slice(padded, (start_zero, top, left), (2, PATCH, PATCH))
        patch = window[0] + 1j * window[1]
        spectra = jnp.fft.fft2(probe * patch[None], norm='ortho')
        intensity = lax.optimization_barrier(jnp.sum(spectra.real ** 2 + spectra.imag ** 2, axis=0))
        ratio = 1.0 - target / jnp.sqrt(jnp.maximum(intensity, 1.0))
        chi = jnp.fft.ifft2(spectra * ratio[None], norm='ortho') * weight
        patch_grad = lax.optimization_barrier(jnp.sum(jnp.conj(probe) * chi, axis=0))
        stacked = jnp.stack([patch_grad.real, patch_grad.imag])
        current = lax.dynamic_slice(gradient, (start_zero, top, left), (2, PATCH, PATCH))
        gradient = lax.dynamic_update_slice(gradient, current + stacked, (start_zero, top, left))
        mode_grad = jnp.conj(patch)[None] * chi
        probe_grad = probe_grad + jnp.stack([mode_grad.real, mode_grad.imag])
        return ((gradient, probe_grad), None)
    initial = (jnp.zeros_like(padded), jnp.zeros_like(probe_modes))
    (gradient, probe_grad), _ = lax.scan(visit, initial, (offsets, measured, active))
    interior = gradient[:, half:half + OBJ_R, half:half + OBJ_C]
    new_object = object_field - 0.25 * interior
    new_probe = probe_modes - 0.5 / math.sqrt(slots) * probe_grad
    return (new_object, new_probe)
```

```python
import math

import jax
import jax.numpy as jnp
import ml_dtypes
import numpy as np
from jax import lax
from jax.experimental import pallas as pl
from jax.experimental.pallas import tpu as pltpu
from jax.sharding import PartitionSpec as P

N = 256
H = 128
MODES = 3
PAD_R = 1280
OBJ_R = 8192
OBJ_C = 4096


def tables():
    n = np.arange(H)[:, None]
    k = np.arange(H)[None, :]
    out = []
    for odd in (0, 1):
        angle = 2.0 * np.pi * ((n * (2 * k + odd)) % N) / N
        c, s = np.cos(angle) / 16.0, np.sin(angle) / 16.0
        full = np.block([[c, -s], [s, c]])
        for matrix in (full, full.T):
            high = matrix.astype(ml_dtypes.bfloat16)
            low = (matrix - high.astype(np.float64)).astype(ml_dtypes.bfloat16)
            out += [high, low]
    return np.stack(out)


def spread_table():
    matrix = np.zeros((N, N), np.float32)
    matrix[np.arange(0, N, 2), np.arange(H)] = 1.0
    matrix[np.arange(1, N, 2), np.arange(H) + H] = 1.0
    return matrix.astype(ml_dtypes.bfloat16)


def split(x):
    high = x.astype(jnp.bfloat16)
    return high, (x - high.astype(jnp.float32)).astype(jnp.bfloat16)


def mm(a, b):
    return jnp.dot(a, b, preferred_element_type=jnp.float32)


def by_right(x, high, low):
    xh, xl = split(x)
    return mm(jnp.concatenate([xh, xl, xh], axis=1), jnp.concatenate([high, high, low], axis=0))


def by_left(high, low, x):
    xh, xl = split(x)
    return mm(jnp.concatenate([high, low, high], axis=1), jnp.concatenate([xh, xh, xl], axis=0))


def rows_up(v, shift, row8):
    t = pltpu.roll(v.reshape(N // 8 + 1, 8, N), (8 - shift) % 8, 1)
    return jnp.where(row8 < 8 - shift, t[:-1], t[1:]).reshape(N, N)


def rows_down(v, shift, row8):
    t = pltpu.roll(v.reshape(N // 8, 8, N), shift, 1)
    none = jnp.zeros((1, 8, N), jnp.float32)
    return jnp.where(
        row8 >= shift, jnp.concatenate([t, none], axis=0), jnp.concatenate([none, t], axis=0)
    ).reshape(N + 8, N)


def body(off_ref, cnt_ref, base_ref, pad_ref, probe_ref, amp_ref, tab_ref, spread_ref, g_ref, pg_ref, spec_ref, half_ref):
    g_ref[...] = jnp.zeros_like(g_ref)
    pg_ref[...] = jnp.zeros_like(pg_ref)
    lane = lax.broadcasted_iota(jnp.int32, (N, N), 1)
    sub = lax.broadcasted_iota(jnp.int32, (N, N), 0)

    def visit(s, carry):
        y = off_ref[2 * s]
        x = off_ref[2 * s + 1]
        top = y - base_ref[0] + H
        left = x - base_ref[1] + H
        first = lane >= left
        first_tall = lax.broadcasted_iota(jnp.int32, (N + 8, N), 1) >= left
        row = sub + y
        ok_first = (lane + (base_ref[1] - H) >= 0) & first
        ok_second = (lane + (base_ref[1] + H) < OBJ_C) & (lane < left)
        row_ok = (row >= 0) & (row < OBJ_R)
        shift = top % 8
        low = pl.multiple_of(top - shift, 8)
        tall = pl.ds(low, N + 8)
        row8 = lax.broadcasted_iota(jnp.int32, (1, 8, N), 1)
        parts = []
        for c in range(2):
            a = rows_up(pad_ref[c, tall, 0:N], shift, row8)
            b = rows_up(pad_ref[c, tall, N : 2 * N], shift, row8)
            v = jnp.where(ok_first & row_ok, a, jnp.where(ok_second & row_ok, b, 0.0))
            parts.append(pltpu.roll(v, (N - left) % N, 1))
        pr, pi = parts

        spread = spread_ref[...]
        half_ref[0] = amp_ref[s, :, 0:H]
        half_ref[1] = amp_ref[s, :, H:N]
        amp = jnp.concatenate(
            [jnp.concatenate([half_ref[i, pl.ds(o, H, 2), :] for i in range(2)], axis=1) for o in range(2)], axis=0
        )
        ah, al = split(amp)
        amp = mm(jnp.concatenate([ah, al], axis=1), jnp.concatenate([spread, spread], axis=0))

        power = [0.0, 0.0]
        for m in range(MODES):
            qr, qi = probe_ref[0, m], probe_ref[1, m]
            wr = qr * pr - qi * pi
            wi = qr * pi + qi * pr
            a = jnp.concatenate([wr[:, :H] + wr[:, H:], wi[:, :H] + wi[:, H:]], axis=1)
            b = jnp.concatenate([wr[:, :H] - wr[:, H:], wi[:, :H] - wi[:, H:]], axis=1)
            ye = by_right(a, tab_ref[0], tab_ref[1])
            yo = by_right(b, tab_ref[4], tab_ref[5])
            se, so = ye[:H] + ye[H:], yo[:H] + yo[H:]
            de, do = ye[:H] - ye[H:], yo[:H] - yo[H:]

            def stack(e, o):
                return jnp.concatenate(
                    [jnp.concatenate([e[:, :H], o[:, :H]], axis=1), jnp.concatenate([e[:, H:], o[:, H:]], axis=1)], axis=0
                )

            ze = by_left(tab_ref[2], tab_ref[3], stack(se, so))
            zo = by_left(tab_ref[6], tab_ref[7], stack(de, do))
            spec_ref[m, 0] = ze
            spec_ref[m, 1] = zo
            for i, z in enumerate((ze, zo)):
                power[i] = power[i] + (z[:H] * z[:H] + z[H:] * z[H:])
        ratios = [1.0 - amp[i * H : (i + 1) * H] * lax.rsqrt(jnp.maximum(power[i], 1.0)) for i in range(2)]
        ratios = [jnp.concatenate([r, r], axis=0) for r in ratios]
        gr, gi = 0.0, 0.0
        for m in range(MODES):
            e = by_left(tab_ref[0], tab_ref[1], spec_ref[m, 0] * ratios[0])
            o = by_left(tab_ref[4], tab_ref[5], spec_ref[m, 1] * ratios[1])
            lo, hi = e + o, e - o

            def lanes(k):
                k = slice(k * H, (k + 1) * H)
                return jnp.concatenate(
                    [jnp.concatenate([lo[:H, k], lo[H:, k]], axis=1), jnp.concatenate([hi[:H, k], hi[H:, k]], axis=1)], axis=0
                )

            e = by_right(lanes(0), tab_ref[2], tab_ref[3])
            o = by_right(lanes(1), tab_ref[6], tab_ref[7])
            lo, hi = e + o, e - o
            cr = jnp.concatenate([lo[:, :H], hi[:, :H]], axis=1)
            ci = jnp.concatenate([lo[:, H:], hi[:, H:]], axis=1)
            qr, qi = probe_ref[0, m], probe_ref[1, m]
            gr = gr + (qr * cr + qi * ci)
            gi = gi + (qr * ci - qi * cr)
            pg_ref[0, m] += pr * cr + pi * ci
            pg_ref[1, m] += pr * ci - pi * cr
        for c, g in enumerate((gr, gi)):
            v = rows_down(pltpu.roll(g, left, 1), shift, row8)
            g_ref[c, tall, 0:N] += jnp.where(first_tall, v, 0.0)
            g_ref[c, tall, N : 2 * N] += jnp.where(first_tall, 0.0, v)
        return carry

    lax.fori_loop(0, cnt_ref[0], visit, 0)


def local_step(padded, probe, amp, offsets, count, base):
    vm = pl.BlockSpec(memory_space=pltpu.VMEM)
    sm = pl.BlockSpec(memory_space=pltpu.SMEM)
    return pl.pallas_call(
        body,
        out_shape=(
            jax.ShapeDtypeStruct((2, PAD_R, 2 * N), jnp.float32),
            jax.ShapeDtypeStruct((2, MODES, N, N), jnp.float32),
        ),
        in_specs=[sm, sm, sm, vm, vm, vm, vm, vm],
        out_specs=(vm, vm),
        scratch_shapes=[pltpu.VMEM((MODES, 2, N, N), jnp.float32), pltpu.VMEM((2, N, H), jnp.float32)],
        compiler_params=pltpu.CompilerParams(vmem_limit_bytes=56 * 2**20),
        name="windows",
    )(offsets, count, base, padded, probe, amp, jnp.asarray(tables()), jnp.asarray(spread_table()))


MESH = pl.DeviceIdType.MESH
T = 1024
F32 = jnp.float32
ROWS, COLS = 8, 16
PR = 1536


def push(src, dst, sems, i, where):
    c = pltpu.make_async_remote_copy(
        src_ref=src, dst_ref=dst, send_sem=sems.at[0, i], recv_sem=sems.at[1, i], device_id=where, device_id_type=MESH
    )
    c.start()
    return c


def greet(peers):
    barrier = pltpu.get_barrier_semaphore()
    for p in peers:
        pl.semaphore_signal(barrier, inc=1, device_id=p, device_id_type=MESH)
    pl.semaphore_wait(barrier, len(peers))


def around():
    r, c = lax.axis_index("row"), lax.axis_index("col")
    up, down = ((r + ROWS - 1) % ROWS, c), ((r + 1) % ROWS, c)
    left, right = (r, (c + COLS - 1) % COLS), (r, (c + 1) % COLS)
    return r, c, up, down, left, right


def halo_body(obj, pad, own_sem, sems):
    r, c, up, down, left, right = around()
    greet((up, down, left, right))
    own = pltpu.make_async_copy(obj, pad.at[:, H : H + T, H : H + N], own_sem)
    copies = []
    for rows in ((0, H), (T - H, H), (H, T - N)):
        a, n = rows
        copies.append(push(obj.at[:, a : a + n, H:N], pad.at[:, H + a : H + a + n, 0:H], sems, len(copies), right))
        copies.append(push(obj.at[:, a : a + n, 0:H], pad.at[:, H + a : H + a + n, H + N :], sems, len(copies), left))
    copies.append(push(obj.at[:, T - H : T], pad.at[:, 0:H, H : H + N], sems, 6, down))
    copies.append(push(obj.at[:, 0:H], pad.at[:, H + T :, H : H + N], sems, 7, up))
    own.start()
    for k, lanes in ((0, slice(0, H)), (1, slice(H + N, 2 * N))):
        copies[k].wait_recv()
        copies.append(push(pad.at[:, H:N, lanes], pad.at[:, H + T :, lanes], sems, 8 + 2 * k, up))
        copies[2 + k].wait_recv()
        copies.append(push(pad.at[:, T : T + H, lanes], pad.at[:, 0:H, lanes], sems, 9 + 2 * k, down))
    own.wait()
    for i, copy in enumerate(copies):
        if i >= 4:
            copy.wait_recv()
    for copy in copies:
        copy.wait_send()


def halo(obj, space=pl.ANY):
    spec = pl.BlockSpec(memory_space=space)
    return pl.pallas_call(
        halo_body,
        out_shape=jax.ShapeDtypeStruct((2, PAD_R, 2 * N), F32),
        in_specs=[spec],
        out_specs=spec,
        scratch_shapes=[pltpu.SemaphoreType.DMA, pltpu.SemaphoreType.DMA((2, 12))],
        compiler_params=pltpu.CompilerParams(collective_id=1, has_side_effects=True, vmem_limit_bytes=40 * 2**20),
        name="halo",
    )(obj)


BIG, SMALL = 1024, 512


def finish_body(g, pg, obj, probe, out, newp, edge, from_rows, from_cols, half, acc, rb1, rs1, rb2, rs2, sems):
    r, c, up, down, left, right = around()
    x, core, z, y = r // 2, r % 2, c // 4, c % 4
    partner = (x * 2 + 1 - core, c)
    a, b = x + core * (z - x), z + core * (x - z)

    def dev(a_, b_, y_):
        return ((a_ + core * (b_ - a_)) * 2 + core, (b_ + core * (a_ - b_)) * 4 + y_)

    line_a = [dev((a + d) % 4, b, y) for d in range(1, 4)]
    line_b = [dev(a, (b + d) % 4, y) for d in range(1, 4)]
    by, ay = b * 4 + y, a * 4 + y
    plane_b = [dev(a, (by + d) % 16 // 4, (by + d) % 16 % 4) for d in range(1, 16)]
    plane_a = [dev((ay + d) % 16 // 4, b, (ay + d) % 16 % 4) for d in range(1, 16)]
    extra = [dev((a + d) % 4, b, (y + e) % 4) for d in range(1, 4) for e in range(4)]
    greet(plane_b + extra + [up, down])

    copies = []

    def go(src, dst, where):
        copies.append(push(src, dst, sems, len(copies), where))
        return copies[-1]

    mine = pl.ds(pl.multiple_of(core * H, H), H)
    other = pl.ds(pl.multiple_of((1 - core) * H, H), H)
    row_copies = [
        go(g.at[:, 0:H], from_rows.at[0], up),
        go(g.at[:, H + T :], from_rows.at[1], down),
    ]
    core_copy = go(pg.at[:, other], half, partner)
    col_copies = []

    def to_cols(src, lo, hi):
        col_copies.append(go(src.at[:, :, 0:H], from_cols.at[0, :, lo:hi], left))
        col_copies.append(go(src.at[:, :, H + N :], from_cols.at[1, :, lo:hi], right))

    to_cols(g.at[:, N:T], H, T - H)

    core_copy.wait_recv()
    acc[...] = pg[:, mine] + half[...]
    na, nb = BIG // 4, SMALL // 4
    first = []
    for d in range(1, 4):
        first.append(go(acc.at[pl.ds(pl.multiple_of((a + d) % 4 * na, na), na)], rb1.at[d - 1], line_a[d - 1]))
        first.append(go(acc.at[pl.ds(pl.multiple_of(BIG + (b + d) % 4 * nb, nb), nb)], rs1.at[d - 1], line_b[d - 1]))

    keep_above = (r > 0).astype(F32)
    keep_below = (r < ROWS - 1).astype(F32)
    row_copies[0].wait_recv()
    edge[0] = g[:, T : T + H] + from_rows[0] * keep_below
    row_copies[1].wait_recv()
    edge[1] = g[:, H:N] + from_rows[1] * keep_above
    to_cols(edge.at[0], T - H, T)
    to_cols(edge.at[1], 0, H)

    for copy in first:
        copy.wait_recv()
    ra = pl.multiple_of(a * na, na)
    rb = pl.multiple_of(BIG + b * nb, nb)
    acc[pl.ds(ra, na)] += rb1[0] + rb1[1] + rb1[2]
    acc[pl.ds(rb, nb)] += rs1[0] + rs1[1] + rs1[2]
    ma, mb = na // 16, nb // 16
    second = []
    for d in range(1, 16):
        second.append(go(acc.at[pl.ds(pl.multiple_of(ra + (by + d) % 16 * ma, ma), ma)], rb2.at[d - 1], plane_b[d - 1]))
        second.append(go(acc.at[pl.ds(pl.multiple_of(rb + (ay + d) % 16 * mb, mb), mb)], rs2.at[d - 1], plane_a[d - 1]))

    out[:, 0:H] = obj[:, 0:H] - 0.25 * edge[1, :, :, H : H + N]
    out[:, H : T - H] = obj[:, H : T - H] - 0.25 * g[:, N:T, H : H + N]
    out[:, T - H :] = obj[:, T - H :] - 0.25 * edge[0, :, :, H : H + N]

    for copy in second:
        copy.wait_recv()
    qa = pl.ds(pl.multiple_of(ra + by * ma, ma), ma)
    qb = pl.ds(pl.multiple_of(rb + ay * mb, mb), mb)
    factor = 0.5 / math.sqrt(1024.0)
    newp[qa, mine] = probe[qa, mine] - factor * (acc[qa] + jnp.sum(rb2[...], axis=0))
    newp[qb, mine] = probe[qb, mine] - factor * (acc[qb] + jnp.sum(rs2[...], axis=0))
    third = []
    for d in range(15):
        third.append(go(newp.at[qa, mine], newp.at[qa, mine], plane_b[d]))
        third.append(go(newp.at[qb, mine], newp.at[qb, mine], plane_a[d]))
    for copy in third:
        copy.wait_recv()
    fourth = []
    sa, sb = pl.ds(ra, na), pl.ds(rb, nb)
    for d in range(3):
        fourth.append(go(newp.at[sa, mine], newp.at[sa, mine], line_a[d]))
        fourth.append(go(newp.at[sb, mine], newp.at[sb, mine], line_b[d]))
    for copy in fourth:
        copy.wait_recv()
    last = go(newp.at[:, mine], newp.at[:, mine], partner)

    for copy in col_copies:
        copy.wait_recv()
    keep_left = (c > 0).astype(F32) * 0.25
    keep_right = (c < COLS - 1).astype(F32) * 0.25
    out[:, :, H:N] -= from_cols[0] * keep_right
    out[:, :, 0:H] -= from_cols[1] * keep_left
    last.wait_recv()
    for copy in copies:
        copy.wait_send()


def finish(g, pg, obj, probe):
    vm = pl.BlockSpec(memory_space=pltpu.VMEM)
    na, nb = BIG // 4, SMALL // 4
    out, newp = pl.pallas_call(
        finish_body,
        out_shape=(jax.ShapeDtypeStruct((2, T, N), F32), jax.ShapeDtypeStruct((PR, N), F32)),
        in_specs=[vm] * 4,
        out_specs=(vm, vm),
        scratch_shapes=[
            pltpu.VMEM((2, 2, H, 2 * N), F32),
            pltpu.VMEM((2, 2, H, 2 * N), F32),
            pltpu.VMEM((2, 2, T, H), F32),
            pltpu.VMEM((PR, H), F32),
            pltpu.VMEM((PR, H), F32),
            pltpu.VMEM((3, na, H), F32),
            pltpu.VMEM((3, nb, H), F32),
            pltpu.VMEM((15, na // 16, H), F32),
            pltpu.VMEM((15, nb // 16, H), F32),
            pltpu.SemaphoreType.DMA((2, 82)),
        ],
        compiler_params=pltpu.CompilerParams(collective_id=2, has_side_effects=True, vmem_limit_bytes=56 * 2**20),
        name="finish",
    )(g, pg.reshape(PR, N), obj, probe.reshape(PR, N))
    return out, newp.reshape(probe.shape)


def on_device(object_field, probe_modes, amplitudes, scan_offsets, slot_counts):
    base = jnp.stack([lax.axis_index("row") * T, lax.axis_index("col") * N]).astype(jnp.int32)
    padded = halo(object_field)
    g, pg = local_step(
        padded,
        probe_modes,
        amplitudes.reshape(8, N, N),
        scan_offsets.reshape(16),
        slot_counts.reshape(1),
        base,
    )
    return finish(g, pg, object_field, probe_modes)


def solution(mesh):
    placed = (
        P(None, "row", "col"),
        P(),
        P("row", "col", None, None, None),
        P("row", "col", None, None),
        P("row", "col"),
    )
    return jax.shard_map(
        on_device,
        mesh=mesh,
        in_specs=placed,
        out_specs=(P(None, "row", "col"), P()),
        check_vma=False,
    )
```

```python
import math

import jax
import jax.numpy as jnp
import ml_dtypes
import numpy as np
from jax import lax
from jax.experimental import pallas as pl
from jax.experimental.pallas import tpu as pltpu
from jax.sharding import PartitionSpec as P

N = 256
H = 128
MODES = 3
PAD_R = 1280
T = 1024
SLOTS = 8
ROWS, COLS = 8, 16
MESH = pl.DeviceIdType.MESH
F32 = jnp.float32
BF16 = jnp.bfloat16
OBJ_R = 8192
OBJ_C = 4096


def tables():
    n = np.arange(H)[:, None]
    k = np.arange(H)[None, :]
    out = []
    for odd in (0, 1):
        angle = 2.0 * np.pi * ((n * (2 * k + odd)) % N) / N
        c, s = np.cos(angle) / 16.0, np.sin(angle) / 16.0
        full = np.block([[c, -s], [s, c]])
        for matrix in (full, full.T):
            high = matrix.astype(ml_dtypes.bfloat16)
            low = (matrix - high.astype(np.float64)).astype(ml_dtypes.bfloat16)
            out += [high, low]
    return np.stack(out)


def spread_table():
    matrix = np.zeros((N, N), np.float32)
    matrix[np.arange(0, N, 2), np.arange(H)] = 1.0
    matrix[np.arange(1, N, 2), np.arange(H) + H] = 1.0
    return matrix.astype(ml_dtypes.bfloat16)


def split(x):
    high = x.astype(BF16)
    return high, (x - high.astype(F32)).astype(BF16)


def right(pair, high, low):
    xh, xl = pair
    return jnp.dot(
        jnp.concatenate([xh, xl, xh], axis=1), jnp.concatenate([high, high, low], axis=0), preferred_element_type=F32
    )


def left(high, low, pair):
    xh, xl = pair
    return jnp.dot(
        jnp.concatenate([high, low, high], axis=1), jnp.concatenate([xh, xh, xl], axis=0), preferred_element_type=F32
    )


def beside(a, b):
    return jnp.concatenate([a, b], axis=1)


def above(a, b):
    return jnp.concatenate([a, b], axis=0)


def rows_up(tiles, shift, back, row8):
    t = [pltpu.roll(v, back, 0) for v in tiles]
    return jnp.concatenate([jnp.where(row8 < 8 - shift, p, q) for p, q in zip(t[:-1], t[1:])], axis=0)


def rows_down(v, shift, row8):
    t = pltpu.roll(v.reshape(N // 8, 8, N), shift, 1)
    none = jnp.zeros((1, 8, N), F32)
    return jnp.where(row8[None] >= shift, jnp.concatenate([t, none], axis=0), jnp.concatenate([none, t], axis=0))


GEO = 32
FIRST, SHIFT, LEFT, BACK_ROW, BACK_COL, ROW, PLACES = range(7)
HT, TT, PT = H // 8, T // 8, PAD_R // 8
TALL = 2 * HT + N // 8 + 1


def geometry(scan_offsets):
    off = scan_offsets.reshape(SLOTS, 2)
    top, lft = (off[:, 0] + H) % T, (off[:, 1] + H) % N
    shift = top % 8
    first = top // 8
    places = jnp.clip(jnp.arange(0, PT, 8)[None] - first[:, None] + HT, 0, TALL - 8)
    fixed = jnp.stack([first, shift, lft, (8 - shift) % 8, (N - lft) % N, off[:, 0]], axis=1)
    table = jnp.concatenate([fixed, places], axis=1).astype(jnp.int32)
    return jnp.pad(table, ((0, 0), (0, GEO - table.shape[1]))).reshape(SLOTS * GEO)


def body(
    geo, cnt, obj, probe_hbm, amp_hbm, tab_hbm, spread_hbm,
    out, newp,
    pad, probe, amp, tab, spread, halves, spec, sh, sl, patch, tall, from_rows, from_cols,
    pg, half, acc, rb1, rb2, local, sems,
):
    r, c = lax.axis_index("row"), lax.axis_index("col")
    up, down = ((r + ROWS - 1) % ROWS, c), ((r + 1) % ROWS, c)
    west, east = (r, (c + COLS - 1) % COLS), (r, (c + 1) % COLS)
    x, core, z, y = r // 2, r % 2, c // 4, c % 4
    partner = (x * 2 + 1 - core, c)
    a, b = x + core * (z - x), z + core * (x - z)

    def dev(a_, b_, y_):
        return ((a_ + core * (b_ - a_)) * 2 + core, (b_ + core * (a_ - b_)) * 4 + y_)

    by = b * 4 + y
    line = [dev((a + d) % 4, b, y) for d in range(1, 4)]
    plane = [dev(a, (by + d) % 16 // 4, (by + d) % 16 % 4) for d in range(1, 16)]

    fetch = [
        pltpu.make_async_copy(src, dst, local.at[i])
        for i, (src, dst) in enumerate(
            (
                (obj, pad.at[:, HT : HT + TT, :, H : H + N]),
                (amp_hbm, amp),
                (spread_hbm, spread),
                (probe_hbm, probe),
                (tab_hbm, tab),
                (obj, out),
            )
        )
    ]
    for f in fetch:
        f.start()

    peers = plane + line + [up, down, west, east]
    barrier = pltpu.get_barrier_semaphore()
    for p in peers:
        pl.semaphore_signal(barrier, inc=1, device_id=p, device_id_type=MESH)
    pl.semaphore_wait(barrier, len(peers))

    count, copies_out = [0], []

    def go(src, dst, where):
        i = count[0]
        count[0] += 1
        copy = pltpu.make_async_remote_copy(
            src_ref=src, dst_ref=dst, send_sem=sems.at[0, i], recv_sem=sems.at[1, i], device_id=where, device_id_type=MESH
        )
        copy.start()
        copies_out.append(copy)
        return copy

    cols = []
    for lo, hi in ((0, HT), (TT - HT, TT), (HT, TT - HT)):
        cols.append(go(obj.at[:, lo:hi, :, H:N], pad.at[:, HT + lo : HT + hi, :, 0:H], east))
        cols.append(go(obj.at[:, lo:hi, :, 0:H], pad.at[:, HT + lo : HT + hi, :, H + N :], west))
    rows = [
        go(obj.at[:, TT - HT : TT], pad.at[:, 0:HT, :, H : H + N], down),
        go(obj.at[:, 0:HT], pad.at[:, HT + TT :, :, H : H + N], up),
    ]
    for k, lanes in ((0, slice(0, H)), (1, slice(H + N, 2 * N))):
        cols[k].wait_recv()
        rows.append(go(pad.at[:, HT : 2 * HT, :, lanes], pad.at[:, HT + TT :, :, lanes], up))
        cols[2 + k].wait_recv()
        rows.append(go(pad.at[:, TT : TT + HT, :, lanes], pad.at[:, 0:HT, :, lanes], down))

    fetch[1].wait()
    fetch[2].wait()

    def order(s, carry):
        halves[0] = amp[s, :, 0:H]
        halves[1] = amp[s, :, H:N]
        v = above(*(beside(*(halves[i, pl.ds(o, H, 2), :] for i in range(2))) for o in range(2)))
        vh, vl = split(v)
        amp[s] = jnp.dot(beside(vh, vl), above(spread[...], spread[...]), preferred_element_type=F32)
        tall[s, :, 0:HT] = jnp.zeros((2, HT, 8, N), F32)
        tall[s, :, TALL - HT :] = jnp.zeros((2, HT, 8, N), F32)
        return carry

    lax.fori_loop(0, SLOTS, order, 0)
    for f in (fetch[0], fetch[3], fetch[4], fetch[5]):
        f.wait()
    for copy in rows + cols[4:]:
        copy.wait_recv()
    for copy in rows + cols:
        copy.wait_send()
    del copies_out[:]

    lane = lax.broadcasted_iota(jnp.int32, (N, N), 1)
    sub = lax.broadcasted_iota(jnp.int32, (N, N), 0)
    row8 = lax.broadcasted_iota(jnp.int32, (8, N), 0)
    col0 = c * N - H

    def forward(s, carry):
        g = s * GEO
        first, shift, lft = geo[g + FIRST], geo[g + SHIFT], geo[g + LEFT]
        row = sub + geo[g + ROW]
        row_ok = (row >= 0) & (row < OBJ_R)
        ok_first = row_ok & (lane >= lft) & (lane + col0 >= 0)
        ok_second = row_ok & (lane < lft) & (lane + (col0 + N) < OBJ_C)
        for i in range(2):
            sides = []
            for lanes in (slice(0, N), slice(N, 2 * N)):
                tiles = [pad[i, first + k, :, lanes] for k in range(N // 8 + 1)]
                sides.append(rows_up(tiles, shift, geo[g + BACK_ROW], row8))
            v = jnp.where(ok_first, sides[0], jnp.where(ok_second, sides[1], 0.0))
            patch[s, i] = pltpu.roll(v, geo[g + BACK_COL], 1)
        pr, pi = patch[s, 0], patch[s, 1]
        plus, minus = [], []
        for m in range(MODES):
            qr, qi = probe[0, m], probe[1, m]
            wr = qr * pr - qi * pi
            wi = qr * pi + qi * pr
            plus.append(beside(wr[:, :H] + wr[:, H:], wi[:, :H] + wi[:, H:]))
            minus.append(beside(wr[:, :H] - wr[:, H:], wi[:, :H] - wi[:, H:]))
        ye = right(split(jnp.concatenate(plus, axis=0)), tab[0], tab[1])
        yo = right(split(jnp.concatenate(minus, axis=0)), tab[4], tab[5])
        power = [0.0, 0.0]
        for m in range(MODES):
            k = m * N
            parts = []
            for sign in (1.0, -1.0):
                e = ye[k : k + H] + sign * ye[k + H : k + N]
                o = yo[k : k + H] + sign * yo[k + H : k + N]
                parts.append(above(beside(e[:, :H], o[:, :H]), beside(e[:, H:], o[:, H:])))
            for i, part in enumerate(parts):
                v = left(tab[2 + 4 * i], tab[3 + 4 * i], split(part))
                spec[m, i] = v
                power[i] = power[i] + (v[:H] * v[:H] + v[H:] * v[H:])
        live = jnp.where(jnp.zeros((1, N), jnp.int32) + s < cnt[0, 0], 1.0, 0.0)
        for i in range(2):
            ratio = live * (1.0 - amp[s, i * H : (i + 1) * H] * lax.rsqrt(jnp.maximum(power[i], 1.0)))
            ratio = above(ratio, ratio)
            for m in range(MODES):
                vh, vl = split(spec[m, i] * ratio)
                sh[(s * MODES + m) * 2 + i] = vh
                sl[(s * MODES + m) * 2 + i] = vl
        return carry

    lax.fori_loop(0, SLOTS, forward, 0)

    def inverse(m, slots):
        even, odd = [], []
        for s in slots:
            k = (s * MODES + m) * 2
            e = left(tab[0], tab[1], (sh[k], sl[k]))
            o = left(tab[4], tab[5], (sh[k + 1], sl[k + 1]))
            lo, hi = e + o, e - o
            even += [beside(lo[:H, :H], lo[H:, :H]), beside(hi[:H, :H], hi[H:, :H])]
            odd += [beside(lo[:H, H:], lo[H:, H:]), beside(hi[:H, H:], hi[H:, H:])]
        e = right(split(jnp.concatenate(even, axis=0)), tab[2], tab[3])
        o = right(split(jnp.concatenate(odd, axis=0)), tab[6], tab[7])
        qr, qi = probe[0, m], probe[1, m]
        mode_r, mode_i = 0.0, 0.0
        for i, s in enumerate(slots):
            ee, oo = e[i * N : (i + 1) * N], o[i * N : (i + 1) * N]
            lo, hi = ee + oo, ee - oo
            cr = beside(lo[:, :H], hi[:, :H])
            ci = beside(lo[:, H:], hi[:, H:])
            pr, pi = patch[s, 0], patch[s, 1]
            mode_r = mode_r + (pr * cr + pi * ci)
            mode_i = mode_i + (pr * ci - pi * cr)
            grads = (qr * cr + qi * ci, qr * ci - qi * cr)
            for k, g in enumerate(grads):
                inner = slice(HT, HT + N // 8)
                if m > 0:
                    g = g + tall[s, k, inner].reshape(N, N)
                if m < MODES - 1:
                    tall[s, k, inner] = g.reshape(N // 8, 8, N)
                else:
                    g = pltpu.roll(g, geo[s * GEO + LEFT], 1)
                    tall[s, k, HT : TALL - HT] = rows_down(g, geo[s * GEO + SHIFT], row8)
        pg[m, 0:N] += mode_r
        pg[m, N:] += mode_i

    mine = pl.ds(pl.multiple_of(core * H, H), H)
    other = pl.ds(pl.multiple_of((1 - core) * H, H), H)
    factor = 0.5 / math.sqrt(ROWS * COLS * SLOTS)

    def probe_sum(m):
        copy = go(pg.at[m, :, other], half.at[m], partner)
        yield
        copy.wait_recv()
        acc[m] = pg[m, :, mine] + half[m]
        sent = []
        for d in range(1, 4):
            piece = pl.ds(pl.multiple_of((a + d) % 4 * H, H), H)
            sent.append(go(acc.at[m, piece], rb1.at[m, d - 1], line[d - 1]))
        yield
        for copy in sent:
            copy.wait_recv()
        start = pl.multiple_of(a * H, H)
        acc[m, pl.ds(start, H)] += rb1[m, 0] + rb1[m, 1] + rb1[m, 2]
        sent = []
        for d in range(1, 16):
            piece = pl.ds(pl.multiple_of(start + (by + d) % 16 * 8, 8), 8)
            sent.append(go(acc.at[m, piece], rb2.at[m, d - 1], plane[d - 1]))
        yield
        for copy in sent:
            copy.wait_recv()
        total = acc[m, pl.ds(pl.multiple_of(start + by * 8, 8), 8)] + jnp.sum(rb2[m], axis=0)
        part, base = a // 2, a % 2 * H
        piece = pl.ds(pl.multiple_of(base + by * 8, 8), 8)
        newp[part, m, piece, mine] = probe[part, m, piece, mine] - factor * total
        ref = newp.at[part, m, piece, mine]
        sent = [go(ref, ref, p) for p in plane]
        yield
        for copy in sent:
            copy.wait_recv()
        ref = newp.at[part, m, pl.ds(pl.multiple_of(base, H), H), mine]
        sent = [go(ref, ref, p) for p in line]
        yield
        for copy in sent:
            copy.wait_recv()
        ref = newp.at[:, m, :, mine]
        copy = go(ref, ref, partner)
        yield
        copy.wait_recv()
        yield

    pg[...] = jnp.zeros_like(pg)
    chains = []
    for m in range(MODES):
        for seg in range(2):

            def two(i, carry, m=m, seg=seg):
                s = seg * 4 + i * 2
                inverse(m, [s, s + 1])
                return carry

            lax.fori_loop(0, 2, two, 0)
            for chain in chains:
                next(chain)
        chains.append(probe_sum(m))
        next(chains[-1])

    half_lane = lax.broadcasted_iota(jnp.int32, (8, 8, N), 2)

    def deposit(lo, hi):
        def block(i, carry):
            k, q = i % 2, i // 2
            first, second = 0.0, 0.0
            for s in range(SLOTS):
                at = geo[s * GEO + PLACES + q]
                v = jnp.stack([tall[s, k, at + j] for j in range(8)])
                w = jnp.where(half_lane >= geo[s * GEO + LEFT], v, 0.0)
                first, second = first + w, second + (v - w)
            pad[k, pl.ds(q * 8, 8), :, 0:N] = first
            pad[k, pl.ds(q * 8, 8), :, N : 2 * N] = second
            return carry

        lax.fori_loop(lo // 4, hi // 4, block, 0)

    def turn():
        for chain in chains:
            next(chain, None)

    from_east, from_west = [], []

    def to_cols(lo, hi):
        from_east.append(go(pad.at[:, HT + lo : HT + hi, :, 0:H], from_cols.at[0, :, lo:hi], west))
        from_west.append(go(pad.at[:, HT + lo : HT + hi, :, H + N :], from_cols.at[1, :, lo:hi], east))

    deposit(0, HT)
    deposit(HT + TT, PT)
    from_below = go(pad.at[:, 0:HT], from_rows.at[0], up)
    from_above = go(pad.at[:, HT + TT :], from_rows.at[1], down)
    turn()
    deposit(2 * HT, TT)
    turn()
    to_cols(HT, TT - HT)
    deposit(HT, 2 * HT)
    deposit(TT, TT + HT)
    from_below.wait_recv()
    pad[:, TT : TT + HT] += from_rows[0] * (r < ROWS - 1).astype(F32)
    from_above.wait_recv()
    pad[:, HT : 2 * HT] += from_rows[1] * (r > 0).astype(F32)
    to_cols(0, HT)
    to_cols(TT - HT, TT)
    for _ in range(6):
        turn()
    out[...] -= 0.25 * pad[:, HT : HT + TT, :, H : H + N]
    for copy in from_east:
        copy.wait_recv()
    out[:, :, :, H:N] -= from_cols[0] * ((c < COLS - 1).astype(F32) * 0.25)
    for copy in from_west:
        copy.wait_recv()
    out[:, :, :, 0:H] -= from_cols[1] * ((c > 0).astype(F32) * 0.25)
    for copy in copies_out:
        copy.wait_send()


def on_device(object_field, probe_modes, amplitudes, scan_offsets, slot_counts):
    hbm = pl.BlockSpec(memory_space=pl.ANY)
    sm = pl.BlockSpec(memory_space=pltpu.SMEM)
    vm = pl.BlockSpec(memory_space=pltpu.VMEM)
    new_object, new_probe = pl.pallas_call(
        body,
        out_shape=(
            jax.ShapeDtypeStruct((2, TT, 8, N), F32),
            jax.ShapeDtypeStruct((2, MODES, N, N), F32),
        ),
        in_specs=[sm, sm, hbm, hbm, hbm, hbm, hbm],
        out_specs=(vm, vm),
        scratch_shapes=[
            pltpu.VMEM((2, PT, 8, 2 * N), F32),
            pltpu.VMEM((2, MODES, N, N), F32),
            pltpu.VMEM((SLOTS, N, N), F32),
            pltpu.VMEM((8, N, N), BF16),
            pltpu.VMEM((N, N), BF16),
            pltpu.VMEM((2, N, H), F32),
            pltpu.VMEM((MODES, 2, N, N), F32),
            pltpu.VMEM((SLOTS * MODES * 2, N, N), BF16),
            pltpu.VMEM((SLOTS * MODES * 2, N, N), BF16),
            pltpu.VMEM((SLOTS, 2, N, N), F32),
            pltpu.VMEM((SLOTS, 2, TALL, 8, N), F32),
            pltpu.VMEM((2, 2, HT, 8, 2 * N), F32),
            pltpu.VMEM((2, 2, TT, 8, H), F32),
            pltpu.VMEM((MODES, 2 * N, N), F32),
            pltpu.VMEM((MODES, 2 * N, H), F32),
            pltpu.VMEM((MODES, 2 * N, H), F32),
            pltpu.VMEM((MODES, 3, H, H), F32),
            pltpu.VMEM((MODES, 15, 8, H), F32),
            pltpu.SemaphoreType.DMA((6,)),
            pltpu.SemaphoreType.DMA((2, 12 + 8 + 38 * MODES)),
        ],
        compiler_params=pltpu.CompilerParams(
            collective_id=1, has_side_effects=True, vmem_limit_bytes=58 * 2**20
        ),
        name="step",
    )(
        geometry(scan_offsets),
        slot_counts,
        object_field.reshape(2, TT, 8, N),
        probe_modes,
        amplitudes.reshape(SLOTS, N, N),
        jnp.asarray(tables()),
        jnp.asarray(spread_table()),
    )
    return new_object.reshape(object_field.shape), new_probe


def solution(mesh):
    placed = (
        P(None, "row", "col"),
        P(),
        P("row", "col", None, None, None),
        P("row", "col", None, None),
        P("row", "col"),
    )
    return jax.shard_map(
        on_device,
        mesh=mesh,
        in_specs=placed,
        out_specs=(P(None, "row", "col"), P()),
        check_vma=False,
    )
```

```python
import math

import jax
import jax.numpy as jnp
import ml_dtypes
import numpy as np
from jax import lax
from jax.experimental import pallas as pl
from jax.experimental.pallas import tpu as pltpu
from jax.sharding import PartitionSpec as P

N = 256
H = 128
MODES = 3
PAD_R = 1280
T = 1024
SLOTS = 8
ROWS, COLS = 8, 16
MESH = pl.DeviceIdType.MESH
F32 = jnp.float32
BF16 = jnp.bfloat16
OBJ_R = 8192
OBJ_C = 4096


def tables():
    n = np.arange(H)[:, None]
    k = np.arange(H)[None, :]
    out = []
    for odd in (0, 1):
        angle = 2.0 * np.pi * ((n * (2 * k + odd)) % N) / N
        c, s = np.cos(angle) / 16.0, np.sin(angle) / 16.0
        full = np.block([[c, -s], [s, c]])
        for matrix in (full, full.T):
            high = matrix.astype(ml_dtypes.bfloat16)
            low = (matrix - high.astype(np.float64)).astype(ml_dtypes.bfloat16)
            out += [high, low]
    return np.stack(out)


def spread_table():
    matrix = np.zeros((N, N), np.float32)
    matrix[np.arange(0, N, 2), np.arange(H)] = 1.0
    matrix[np.arange(1, N, 2), np.arange(H) + H] = 1.0
    return matrix.astype(ml_dtypes.bfloat16)


def split(x):
    high = x.astype(BF16)
    return high, (x - high.astype(F32)).astype(BF16)


def right(pair, high, low):
    xh, xl = pair
    return jnp.dot(
        jnp.concatenate([xh, xl, xh], axis=1), jnp.concatenate([high, high, low], axis=0), preferred_element_type=F32
    )


def left(high, low, pair):
    xh, xl = pair
    return jnp.dot(
        jnp.concatenate([high, low, high], axis=1), jnp.concatenate([xh, xh, xl], axis=0), preferred_element_type=F32
    )


def beside(a, b):
    return jnp.concatenate([a, b], axis=1)


def above(a, b):
    return jnp.concatenate([a, b], axis=0)


def rows_up(tiles, shift, back, row8):
    t = [pltpu.roll(v, back, 0) for v in tiles]
    return jnp.concatenate([jnp.where(row8 < 8 - shift, p, q) for p, q in zip(t[:-1], t[1:])], axis=0)


def rows_down(v, shift, row8):
    t = pltpu.roll(v.reshape(N // 8, 8, N), shift, 1)
    none = jnp.zeros((1, 8, N), F32)
    return jnp.where(row8[None] >= shift, jnp.concatenate([t, none], axis=0), jnp.concatenate([none, t], axis=0))


GEO = 32
FIRST, SHIFT, LEFT, BACK_ROW, BACK_COL, ROW, PLACES = range(7)
HT, TT, PT = H // 8, T // 8, PAD_R // 8
EDGE = 8
TALL = 2 * EDGE + N // 8 + 1


def geometry(scan_offsets):
    off = scan_offsets.reshape(SLOTS, 2)
    top, lft = (off[:, 0] + H) % T, (off[:, 1] + H) % N
    shift = top % 8
    first = top // 8
    places = jnp.clip(jnp.arange(0, PT, 8)[None] - first[:, None] + EDGE, 0, TALL - 8)
    fixed = jnp.stack([first, shift, lft, (8 - shift) % 8, (N - lft) % N, off[:, 0]], axis=1)
    table = jnp.concatenate([fixed, places], axis=1).astype(jnp.int32)
    return jnp.pad(table, ((0, 0), (0, GEO - table.shape[1]))).reshape(SLOTS * GEO)


def body(
    geo, cnt, obj, probe_hbm, amp_hbm, tab_hbm, spread_hbm,
    out, newp,
    pad, probe, amp, tab, spread, halves, spec, sh, sl, patch, tall, from_rows, from_cols,
    pg, half, acc, rb1, rb2, local, sems,
):
    r, c = lax.axis_index("row"), lax.axis_index("col")
    up, down = ((r + ROWS - 1) % ROWS, c), ((r + 1) % ROWS, c)
    west, east = (r, (c + COLS - 1) % COLS), (r, (c + 1) % COLS)
    x, core, z, y = r // 2, r % 2, c // 4, c % 4
    partner = (x * 2 + 1 - core, c)
    a, b = x + core * (z - x), z + core * (x - z)

    def dev(a_, b_, y_):
        return ((a_ + core * (b_ - a_)) * 2 + core, (b_ + core * (a_ - b_)) * 4 + y_)

    by = b * 4 + y
    line = [dev((a + d) % 4, b, y) for d in range(1, 4)]
    plane = [dev(a, (by + d) % 16 // 4, (by + d) % 16 % 4) for d in range(1, 16)]

    fetch = [
        pltpu.make_async_copy(src, dst, local.at[i])
        for i, (src, dst) in enumerate(
            (
                (obj, pad.at[:, HT : HT + TT, :, H : H + N]),
                (amp_hbm, amp),
                (spread_hbm, spread),
                (probe_hbm, probe),
                (tab_hbm, tab),
                (obj, out),
            )
        )
    ]
    for f in fetch:
        f.start()

    peers = plane + line + [up, down, west, east]
    barrier = pltpu.get_barrier_semaphore()
    for p in peers:
        pl.semaphore_signal(barrier, inc=1, device_id=p, device_id_type=MESH)
    pl.semaphore_wait(barrier, len(peers))

    count, copies_out = [0], []

    def go(src, dst, where):
        i = count[0]
        count[0] += 1
        copy = pltpu.make_async_remote_copy(
            src_ref=src, dst_ref=dst, send_sem=sems.at[0, i], recv_sem=sems.at[1, i], device_id=where, device_id_type=MESH
        )
        copy.start()
        copies_out.append(copy)
        return copy

    cols = []
    for lo, hi in ((0, HT), (TT - HT, TT), (HT, TT - HT)):
        cols.append(go(obj.at[:, lo:hi, :, H:N], pad.at[:, HT + lo : HT + hi, :, 0:H], east))
        cols.append(go(obj.at[:, lo:hi, :, 0:H], pad.at[:, HT + lo : HT + hi, :, H + N :], west))
    rows = [
        go(obj.at[:, TT - HT : TT], pad.at[:, 0:HT, :, H : H + N], down),
        go(obj.at[:, 0:HT], pad.at[:, HT + TT :, :, H : H + N], up),
    ]
    for k, lanes in ((0, slice(0, H)), (1, slice(H + N, 2 * N))):
        cols[k].wait_recv()
        rows.append(go(pad.at[:, HT : 2 * HT, :, lanes], pad.at[:, HT + TT :, :, lanes], up))
        cols[2 + k].wait_recv()
        rows.append(go(pad.at[:, TT : TT + HT, :, lanes], pad.at[:, 0:HT, :, lanes], down))

    fetch[1].wait()
    fetch[2].wait()

    def order(s, carry):
        halves[0] = amp[s, :, 0:H]
        halves[1] = amp[s, :, H:N]
        v = above(*(beside(*(halves[i, pl.ds(o, H, 2), :] for i in range(2))) for o in range(2)))
        vh, vl = split(v)
        amp[s] = jnp.dot(beside(vh, vl), above(spread[...], spread[...]), preferred_element_type=F32)
        tall[s, :, 0:EDGE] = jnp.zeros((2, EDGE, 8, 2 * N), F32)
        tall[s, :, TALL - EDGE :] = jnp.zeros((2, EDGE, 8, 2 * N), F32)
        return carry

    lax.fori_loop(0, SLOTS, order, 0)
    for f in (fetch[0], fetch[3], fetch[4], fetch[5]):
        f.wait()
    for copy in rows + cols[4:]:
        copy.wait_recv()
    for copy in rows + cols:
        copy.wait_send()
    del copies_out[:]

    lane = lax.broadcasted_iota(jnp.int32, (N, N), 1)
    sub = lax.broadcasted_iota(jnp.int32, (N, N), 0)
    row8 = lax.broadcasted_iota(jnp.int32, (8, N), 0)
    lane33 = lax.broadcasted_iota(jnp.int32, (N // 8 + 1, 8, N), 2)
    col0 = c * N - H

    def forward(s, carry):
        g = s * GEO
        first, shift, lft = geo[g + FIRST], geo[g + SHIFT], geo[g + LEFT]
        row = sub + geo[g + ROW]
        row_ok = (row >= 0) & (row < OBJ_R)
        ok_first = row_ok & (lane >= lft) & (lane + col0 >= 0)
        ok_second = row_ok & (lane < lft) & (lane + (col0 + N) < OBJ_C)
        for i in range(2):
            sides = []
            for lanes in (slice(0, N), slice(N, 2 * N)):
                tiles = [pad[i, first + k, :, lanes] for k in range(N // 8 + 1)]
                sides.append(rows_up(tiles, shift, geo[g + BACK_ROW], row8))
            v = jnp.where(ok_first, sides[0], jnp.where(ok_second, sides[1], 0.0))
            patch[s, i] = pltpu.roll(v, geo[g + BACK_COL], 1)
        pr, pi = patch[s, 0], patch[s, 1]
        plus, minus = [], []
        for m in range(MODES):
            qr, qi = probe[0, m], probe[1, m]
            wr = qr * pr - qi * pi
            wi = qr * pi + qi * pr
            plus.append(beside(wr[:, :H] + wr[:, H:], wi[:, :H] + wi[:, H:]))
            minus.append(beside(wr[:, :H] - wr[:, H:], wi[:, :H] - wi[:, H:]))
        ye = right(split(jnp.concatenate(plus, axis=0)), tab[0], tab[1])
        yo = right(split(jnp.concatenate(minus, axis=0)), tab[4], tab[5])
        power = [0.0, 0.0]
        for m in range(MODES):
            k = m * N
            parts = []
            for sign in (1.0, -1.0):
                e = ye[k : k + H] + sign * ye[k + H : k + N]
                o = yo[k : k + H] + sign * yo[k + H : k + N]
                parts.append(above(beside(e[:, :H], o[:, :H]), beside(e[:, H:], o[:, H:])))
            for i, part in enumerate(parts):
                v = left(tab[2 + 4 * i], tab[3 + 4 * i], split(part))
                spec[m, i] = v
                power[i] = power[i] + (v[:H] * v[:H] + v[H:] * v[H:])
        live = jnp.where(jnp.zeros((1, N), jnp.int32) + s < cnt[0, 0], 1.0, 0.0)
        for i in range(2):
            ratio = live * (1.0 - amp[s, i * H : (i + 1) * H] * lax.rsqrt(jnp.maximum(power[i], 1.0)))
            ratio = above(ratio, ratio)
            for m in range(MODES):
                vh, vl = split(spec[m, i] * ratio)
                sh[(s * MODES + m) * 2 + i] = vh
                sl[(s * MODES + m) * 2 + i] = vl
        return carry

    lax.fori_loop(0, SLOTS, forward, 0)

    def inverse(m, slots):
        even, odd = [], []
        for s in slots:
            k = (s * MODES + m) * 2
            e = left(tab[0], tab[1], (sh[k], sl[k]))
            o = left(tab[4], tab[5], (sh[k + 1], sl[k + 1]))
            lo, hi = e + o, e - o
            even += [beside(lo[:H, :H], lo[H:, :H]), beside(hi[:H, :H], hi[H:, :H])]
            odd += [beside(lo[:H, H:], lo[H:, H:]), beside(hi[:H, H:], hi[H:, H:])]
        e = right(split(jnp.concatenate(even, axis=0)), tab[2], tab[3])
        o = right(split(jnp.concatenate(odd, axis=0)), tab[6], tab[7])
        qr, qi = probe[0, m], probe[1, m]
        mode_r, mode_i = 0.0, 0.0
        for i, s in enumerate(slots):
            ee, oo = e[i * N : (i + 1) * N], o[i * N : (i + 1) * N]
            lo, hi = ee + oo, ee - oo
            cr = beside(lo[:, :H], hi[:, :H])
            ci = beside(lo[:, H:], hi[:, H:])
            pr, pi = patch[s, 0], patch[s, 1]
            mode_r = mode_r + (pr * cr + pi * ci)
            mode_i = mode_i + (pr * ci - pi * cr)
            grads = (qr * cr + qi * ci, qr * ci - qi * cr)
            for k, g in enumerate(grads):
                inner = slice(EDGE, EDGE + N // 8)
                if m > 0:
                    g = g + tall[s, k, inner, :, 0:N].reshape(N, N)
                if m < MODES - 1:
                    tall[s, k, inner, :, 0:N] = g.reshape(N // 8, 8, N)
                else:
                    lft = geo[s * GEO + LEFT]
                    g = rows_down(pltpu.roll(g, lft, 1), geo[s * GEO + SHIFT], row8)
                    first = jnp.where(lane33 >= lft, g, 0.0)
                    tall[s, k, EDGE : TALL - EDGE, :, 0:N] = first
                    tall[s, k, EDGE : TALL - EDGE, :, N : 2 * N] = g - first
        pg[m, 0:N] += mode_r
        pg[m, N:] += mode_i

    mine = pl.ds(pl.multiple_of(core * H, H), H)
    other = pl.ds(pl.multiple_of((1 - core) * H, H), H)
    factor = 0.5 / math.sqrt(ROWS * COLS * SLOTS)

    def probe_sum(m):
        copy = go(pg.at[m, :, other], half.at[m], partner)
        yield
        copy.wait_recv()
        acc[m] = pg[m, :, mine] + half[m]
        sent = []
        for d in range(1, 4):
            piece = pl.ds(pl.multiple_of((a + d) % 4 * H, H), H)
            sent.append(go(acc.at[m, piece], rb1.at[m, d - 1], line[d - 1]))
        yield
        for copy in sent:
            copy.wait_recv()
        start = pl.multiple_of(a * H, H)
        acc[m, pl.ds(start, H)] += rb1[m, 0] + rb1[m, 1] + rb1[m, 2]
        sent = []
        for d in range(1, 16):
            piece = pl.ds(pl.multiple_of(start + (by + d) % 16 * 8, 8), 8)
            sent.append(go(acc.at[m, piece], rb2.at[m, d - 1], plane[d - 1]))
        yield
        for copy in sent:
            copy.wait_recv()
        total = acc[m, pl.ds(pl.multiple_of(start + by * 8, 8), 8)] + jnp.sum(rb2[m], axis=0)
        part, base = a // 2, a % 2 * H
        piece = pl.ds(pl.multiple_of(base + by * 8, 8), 8)
        newp[part, m, piece, mine] = probe[part, m, piece, mine] - factor * total
        ref = newp.at[part, m, piece, mine]
        sent = [go(ref, ref, p) for p in plane]
        yield
        for copy in sent:
            copy.wait_recv()
        ref = newp.at[part, m, pl.ds(pl.multiple_of(base, H), H), mine]
        sent = [go(ref, ref, p) for p in line]
        yield
        for copy in sent:
            copy.wait_recv()
        ref = newp.at[:, m, :, mine]
        copy = go(ref, ref, partner)
        yield
        copy.wait_recv()
        yield

    pg[...] = jnp.zeros_like(pg)
    chains = []
    for m in range(MODES):
        for seg in range(2):

            def two(i, carry, m=m, seg=seg):
                s = seg * 4 + i * 2
                inverse(m, [s, s + 1])
                return carry

            lax.fori_loop(0, 2, two, 0)
            for chain in chains:
                next(chain)
        chains.append(probe_sum(m))
        next(chains[-1])

    def deposit(lo, hi):
        def block(q, carry):
            for k in range(2):
                total = [0.0] * 8
                for s in range(SLOTS):
                    at = geo[s * GEO + PLACES + q]
                    total = [total[j] + tall[s, k, at + j] for j in range(8)]
                pad[k, pl.ds(q * 8, 8)] = jnp.stack(total)
            return carry

        lax.fori_loop(lo // 8, hi // 8, block, 0)

    def turn():
        for chain in chains:
            next(chain, None)

    from_east, from_west = [], []

    def to_cols(lo, hi):
        from_east.append(go(pad.at[:, HT + lo : HT + hi, :, 0:H], from_cols.at[0, :, lo:hi], west))
        from_west.append(go(pad.at[:, HT + lo : HT + hi, :, H + N :], from_cols.at[1, :, lo:hi], east))

    deposit(0, HT)
    deposit(HT + TT, PT)
    from_below = go(pad.at[:, 0:HT], from_rows.at[0], up)
    from_above = go(pad.at[:, HT + TT :], from_rows.at[1], down)
    turn()
    deposit(2 * HT, TT)
    to_cols(HT, HT + 24)
    deposit(HT, 2 * HT)
    deposit(TT, TT + HT)
    turn()
    to_cols(HT + 24, HT + 48)
    from_below.wait_recv()
    pad[:, TT : TT + HT] += from_rows[0] * (r < ROWS - 1).astype(F32)
    from_above.wait_recv()
    pad[:, HT : 2 * HT] += from_rows[1] * (r > 0).astype(F32)
    turn()
    to_cols(HT + 48, TT - HT)
    to_cols(0, HT)
    to_cols(TT - HT, TT)
    out[...] -= 0.25 * pad[:, HT : HT + TT, :, H : H + N]
    for _ in range(6):
        turn()
    for copy in from_east:
        copy.wait_recv()
    out[:, :, :, H:N] -= from_cols[0] * ((c < COLS - 1).astype(F32) * 0.25)
    for copy in from_west:
        copy.wait_recv()
    out[:, :, :, 0:H] -= from_cols[1] * ((c > 0).astype(F32) * 0.25)
    for copy in copies_out:
        copy.wait_send()


def on_device(object_field, probe_modes, amplitudes, scan_offsets, slot_counts):
    hbm = pl.BlockSpec(memory_space=pl.ANY)
    sm = pl.BlockSpec(memory_space=pltpu.SMEM)
    vm = pl.BlockSpec(memory_space=pltpu.VMEM)
    new_object, new_probe = pl.pallas_call(
        body,
        out_shape=(
            jax.ShapeDtypeStruct((2, TT, 8, N), F32),
            jax.ShapeDtypeStruct((2, MODES, N, N), F32),
        ),
        in_specs=[sm, sm, hbm, hbm, hbm, hbm, hbm],
        out_specs=(vm, vm),
        scratch_shapes=[
            pltpu.VMEM((2, PT, 8, 2 * N), F32),
            pltpu.VMEM((2, MODES, N, N), F32),
            pltpu.VMEM((SLOTS, N, N), F32),
            pltpu.VMEM((8, N, N), BF16),
            pltpu.VMEM((N, N), BF16),
            pltpu.VMEM((2, N, H), F32),
            pltpu.VMEM((MODES, 2, N, N), F32),
            pltpu.VMEM((SLOTS * MODES * 2, N, N), BF16),
            pltpu.VMEM((SLOTS * MODES * 2, N, N), BF16),
            pltpu.VMEM((SLOTS, 2, N, N), F32),
            pltpu.VMEM((SLOTS, 2, TALL, 8, 2 * N), F32),
            pltpu.VMEM((2, 2, HT, 8, 2 * N), F32),
            pltpu.VMEM((2, 2, TT, 8, H), F32),
            pltpu.VMEM((MODES, 2 * N, N), F32),
            pltpu.VMEM((MODES, 2 * N, H), F32),
            pltpu.VMEM((MODES, 2 * N, H), F32),
            pltpu.VMEM((MODES, 3, H, H), F32),
            pltpu.VMEM((MODES, 15, 8, H), F32),
            pltpu.SemaphoreType.DMA((6,)),
            pltpu.SemaphoreType.DMA((2, 12 + 12 + 38 * MODES)),
        ],
        compiler_params=pltpu.CompilerParams(
            collective_id=1, has_side_effects=True, vmem_limit_bytes=58 * 2**20
        ),
        name="step",
    )(
        geometry(scan_offsets),
        slot_counts,
        object_field.reshape(2, TT, 8, N),
        probe_modes,
        amplitudes.reshape(SLOTS, N, N),
        jnp.asarray(tables()),
        jnp.asarray(spread_table()),
    )
    return new_object.reshape(object_field.shape), new_probe


def solution(mesh):
    placed = (
        P(None, "row", "col"),
        P(),
        P("row", "col", None, None, None),
        P("row", "col", None, None),
        P("row", "col"),
    )
    return jax.shard_map(
        on_device,
        mesh=mesh,
        in_specs=placed,
        out_specs=(P(None, "row", "col"), P()),
        check_vma=False,
    )
```

```python
import math

import jax
import jax.numpy as jnp
import ml_dtypes
import numpy as np
from jax import lax
from jax.experimental import pallas as pl
from jax.experimental.pallas import tpu as pltpu
from jax.sharding import PartitionSpec as P

N = 256
H = 128
MODES = 3
PAD_R = 1280
T = 1024
SLOTS = 8
ROWS, COLS = 8, 16
MESH = pl.DeviceIdType.MESH
F32 = jnp.float32
BF16 = jnp.bfloat16
OBJ_R = 8192
OBJ_C = 4096


def tables():
    n = np.arange(H)[:, None]
    k = np.arange(H)[None, :]
    out = []
    for odd in (0, 1):
        angle = 2.0 * np.pi * ((n * (2 * k + odd)) % N) / N
        c, s = np.cos(angle) / 16.0, np.sin(angle) / 16.0
        full = np.block([[c, -s], [s, c]])
        for matrix in (full, full.T):
            high = matrix.astype(ml_dtypes.bfloat16)
            low = (matrix - high.astype(np.float64)).astype(ml_dtypes.bfloat16)
            out += [high, low]
    return np.stack(out)


def spread_table():
    matrix = np.zeros((N, N), np.float32)
    matrix[np.arange(0, N, 2), np.arange(H)] = 1.0
    matrix[np.arange(1, N, 2), np.arange(H) + H] = 1.0
    return matrix.astype(ml_dtypes.bfloat16)


def split(x):
    high = x.astype(BF16)
    return high, (x - high.astype(F32)).astype(BF16)


def right(pair, high, low):
    xh, xl = pair
    return jnp.dot(
        jnp.concatenate([xh, xl, xh], axis=1), jnp.concatenate([high, high, low], axis=0), preferred_element_type=F32
    )


def left(high, low, pair):
    xh, xl = pair
    return jnp.dot(
        jnp.concatenate([high, low, high], axis=1), jnp.concatenate([xh, xh, xl], axis=0), preferred_element_type=F32
    )


def beside(a, b):
    return jnp.concatenate([a, b], axis=1)


def above(a, b):
    return jnp.concatenate([a, b], axis=0)


def rows_up(tiles, shift, back, row8):
    t = [pltpu.roll(v, back, 0) for v in tiles]
    return jnp.concatenate([jnp.where(row8 < 8 - shift, p, q) for p, q in zip(t[:-1], t[1:])], axis=0)


def rows_down(v, shift, row8):
    t = pltpu.roll(v.reshape(N // 8, 8, N), shift, 1)
    none = jnp.zeros((1, 8, N), F32)
    return jnp.where(row8[None] >= shift, jnp.concatenate([t, none], axis=0), jnp.concatenate([none, t], axis=0))


GEO = 32
FIRST, SHIFT, LEFT, BACK_ROW, BACK_COL, ROW, PLACES = range(7)
HT, TT, PT = H // 8, T // 8, PAD_R // 8
EDGE = 8
TALL = 2 * EDGE + N // 8 + 1


def geometry(scan_offsets):
    off = scan_offsets.reshape(SLOTS, 2)
    top, lft = (off[:, 0] + H) % T, (off[:, 1] + H) % N
    shift = top % 8
    first = top // 8
    places = jnp.clip(jnp.arange(0, PT, 8)[None] - first[:, None] + EDGE, 0, TALL - 8)
    fixed = jnp.stack([first, shift, lft, (8 - shift) % 8, (N - lft) % N, off[:, 0]], axis=1)
    table = jnp.concatenate([fixed, places], axis=1).astype(jnp.int32)
    return jnp.pad(table, ((0, 0), (0, GEO - table.shape[1]))).reshape(SLOTS * GEO)


def body(
    geo, cnt, obj, obj_flat, probe_hbm, amp_hbm, tab_hbm, spread_hbm,
    out, newp,
    pad, probe, tab, spread, halves, spec_a, spec_b, wave_a, wave_b, sh, sl, patch, tall, from_rows, from_cols,
    pg, half, rb1, rb2, rb3, local, sems,
):
    r, c = lax.axis_index("row"), lax.axis_index("col")
    up, down = ((r + ROWS - 1) % ROWS, c), ((r + 1) % ROWS, c)
    west, east = (r, (c + COLS - 1) % COLS), (r, (c + 1) % COLS)
    x, core, z, y = r // 2, r % 2, c // 4, c % 4
    partner = (x * 2 + 1 - core, c)
    a, b = x, z

    def dev(a_, b_, y_):
        return (a_ * 2 + core, b_ * 4 + y_)

    line_a = [dev((a + d) % 4, b, y) for d in range(1, 4)]
    line_b = [dev(a, (b + d) % 4, y) for d in range(1, 4)]
    line_y = [dev(a, b, (y + d) % 4) for d in range(1, 4)]

    fetch = [
        pltpu.make_async_copy(src, dst, local.at[i])
        for i, (src, dst) in enumerate(
            (
                (obj, pad.at[:, HT : HT + TT, :, H : H + N]),
                (amp_hbm, out),
                (spread_hbm, spread),
                (probe_hbm, probe),
                (tab_hbm, tab),
            )
        )
    ]
    for f in fetch:
        f.start()

    peers = line_a + line_b + line_y + [up, down, west, east]
    barrier = pltpu.get_barrier_semaphore()
    for p in peers:
        pl.semaphore_signal(barrier, inc=1, device_id=p, device_id_type=MESH)
    pl.semaphore_wait(barrier, len(peers))

    count, copies_out = [0], []

    def go(src, dst, where):
        i = count[0]
        count[0] += 1
        copy = pltpu.make_async_remote_copy(
            src_ref=src, dst_ref=dst, send_sem=sems.at[0, i], recv_sem=sems.at[1, i], device_id=where, device_id_type=MESH
        )
        copy.start()
        copies_out.append(copy)
        return copy

    cols = []
    for lo, hi in ((0, HT), (TT - HT, TT), (HT, TT - HT)):
        cols.append(go(obj.at[:, lo:hi, :, H:N], pad.at[:, HT + lo : HT + hi, :, 0:H], east))
        cols.append(go(obj.at[:, lo:hi, :, 0:H], pad.at[:, HT + lo : HT + hi, :, H + N :], west))
    rows = [
        go(obj.at[:, TT - HT : TT], pad.at[:, 0:HT, :, H : H + N], down),
        go(obj.at[:, 0:HT], pad.at[:, HT + TT :, :, H : H + N], up),
    ]
    for k, lanes in ((0, slice(0, H)), (1, slice(H + N, 2 * N))):
        cols[k].wait_recv()
        rows.append(go(pad.at[:, HT : 2 * HT, :, lanes], pad.at[:, HT + TT :, :, lanes], up))
        cols[2 + k].wait_recv()
        rows.append(go(pad.at[:, TT : TT + HT, :, lanes], pad.at[:, 0:HT, :, lanes], down))

    fetch[1].wait()
    fetch[2].wait()

    def order(s, carry):
        halves[0] = out[s, :, 0:H]
        halves[1] = out[s, :, H:N]
        v = above(*(beside(*(halves[i, pl.ds(o, H, 2), :] for i in range(2))) for o in range(2)))
        vh, vl = split(v)
        out[s] = jnp.dot(beside(vh, vl), above(spread[...], spread[...]), preferred_element_type=F32)
        tall[s] = jnp.zeros((2, TALL, 8, 2 * N), F32)
        return carry

    lax.fori_loop(0, SLOTS, order, 0)
    for f in (fetch[0], fetch[3], fetch[4]):
        f.wait()
    for copy in rows + cols[4:]:
        copy.wait_recv()
    for copy in rows + cols:
        copy.wait_send()
    del copies_out[:]

    lane = lax.broadcasted_iota(jnp.int32, (N, N), 1)
    sub = lax.broadcasted_iota(jnp.int32, (N, N), 0)
    row8 = lax.broadcasted_iota(jnp.int32, (8, N), 0)
    lane33 = lax.broadcasted_iota(jnp.int32, (N // 8 + 1, 8, N), 2)
    col0 = c * N - H

    def window(s, wave):
        g = s * GEO
        first, shift, lft = geo[g + FIRST], geo[g + SHIFT], geo[g + LEFT]
        row = sub + geo[g + ROW]
        row_ok = (row >= 0) & (row < OBJ_R)
        ok_first = row_ok & (lane >= lft) & (lane + col0 >= 0)
        ok_second = row_ok & (lane < lft) & (lane + (col0 + N) < OBJ_C)
        parts = []
        for i in range(2):
            sides = []
            for lanes in (slice(0, N), slice(N, 2 * N)):
                tiles = [pad[i, first + k, :, lanes] for k in range(N // 8 + 1)]
                sides.append(rows_up(tiles, shift, geo[g + BACK_ROW], row8))
            v = jnp.where(ok_first, sides[0], jnp.where(ok_second, sides[1], 0.0))
            parts.append(pltpu.roll(v, geo[g + BACK_COL], 1))
        pr, pi = parts
        patch[s, 0] = pr
        patch[s, 1] = pi
        for m in range(MODES):
            qr, qi = probe[0, m], probe[1, m]
            wr = qr * pr - qi * pi
            wi = qr * pi + qi * pr
            rows = slice(m * N, (m + 1) * N)
            plus = beside(wr[:, :H] + wr[:, H:], wi[:, :H] + wi[:, H:])
            wave[0, 0, rows], wave[0, 1, rows] = split(plus)
            minus = beside(wr[:, :H] - wr[:, H:], wi[:, :H] - wi[:, H:])
            wave[1, 0, rows], wave[1, 1, rows] = split(minus)

    def transform(wave, spec):
        ye = right((wave[0, 0], wave[0, 1]), tab[0], tab[1])
        yo = right((wave[1, 0], wave[1, 1]), tab[4], tab[5])
        for m in range(MODES):
            k = m * N
            for i, sign in enumerate((1.0, -1.0)):
                e = ye[k : k + H] + sign * ye[k + H : k + N]
                o = yo[k : k + H] + sign * yo[k + H : k + N]
                part = above(beside(e[:, :H], o[:, :H]), beside(e[:, H:], o[:, H:]))
                spec[m, i] = left(tab[2 + 4 * i], tab[3 + 4 * i], split(part))

    def scale(s, spec):
        live = jnp.where(s < cnt[0, 0], 1.0, 0.0)
        for i in range(2):
            power = 0.0
            for m in range(MODES):
                v = spec[m, i]
                power = power + (v[:H] * v[:H] + v[H:] * v[H:])
            ratio = live * (1.0 - out[s, i * H : (i + 1) * H] * lax.rsqrt(jnp.maximum(power, 1.0)))
            ratio = above(ratio, ratio)
            for m in range(MODES):
                k = (s * MODES + m) * 2 + i
                sh[k], sl[k] = split(spec[m, i] * ratio)

    def two_slots(q, carry):
        s = 2 * q
        transform(wave_a, spec_a)
        window(s + 1, wave_b)
        scale((s + SLOTS - 1) % SLOTS, spec_b)
        transform(wave_b, spec_b)
        window((s + 2) % SLOTS, wave_a)
        scale(s, spec_a)
        return carry

    spec_b[...] = jnp.zeros_like(spec_b)
    window(0, wave_a)
    lax.fori_loop(0, SLOTS // 2, two_slots, 0)
    scale(SLOTS - 1, spec_b)
    again = pltpu.make_async_copy(obj_flat, out, local.at[5])
    again.start()

    PAIRS = SLOTS // 2

    def back(p, spec):
        m, j = p // PAIRS, p % PAIRS
        even, odd = [], []
        for t in range(2):
            k = ((2 * j + t) * MODES + m) * 2
            e = left(tab[0], tab[1], (sh[k], sl[k]))
            o = left(tab[4], tab[5], (sh[k + 1], sl[k + 1]))
            lo, hi = e + o, e - o
            even += [beside(lo[:H, :H], lo[H:, :H]), beside(hi[:H, :H], hi[H:, :H])]
            odd += [beside(lo[:H, H:], lo[H:, H:]), beside(hi[:H, H:], hi[H:, H:])]
        e = right(split(jnp.concatenate(even, axis=0)), tab[2], tab[3])
        o = right(split(jnp.concatenate(odd, axis=0)), tab[6], tab[7])
        for t in range(2):
            spec[t, 0] = e[t * N : (t + 1) * N]
            spec[t, 1] = o[t * N : (t + 1) * N]

    inner = slice(EDGE, EDGE + N // 8)

    def collect(p, spec):
        m, j = p // PAIRS, p % PAIRS
        mode_r, mode_i = 0.0, 0.0
        qr, qi = probe[0, m], probe[1, m]
        for t in range(2):
            s = 2 * j + t
            ee, oo = spec[t, 0], spec[t, 1]
            lo, hi = ee + oo, ee - oo
            cr = beside(lo[:, :H], hi[:, :H])
            ci = beside(lo[:, H:], hi[:, H:])
            pr, pi = patch[s, 0], patch[s, 1]
            mode_r = mode_r + (pr * cr + pi * ci)
            mode_i = mode_i + (pr * ci - pi * cr)
            for k, g in enumerate((qr * cr + qi * ci, qr * ci - qi * cr)):
                tall[s, k, inner, :, 0:N] += g.reshape(N // 8, 8, N)
        pg[m, 0:N] += mode_r
        pg[m, N:] += mode_i

    def settle(s, carry):
        lft = geo[s * GEO + LEFT]
        for k in range(2):
            g = pltpu.roll(tall[s, k, inner, :, 0:N].reshape(N, N), lft, 1)
            g = rows_down(g, geo[s * GEO + SHIFT], row8)
            first = jnp.where(lane33 >= lft, g, 0.0)
            tall[s, k, EDGE : TALL - EDGE, :, 0:N] = first
            tall[s, k, EDGE : TALL - EDGE, :, N : 2 * N] = g - first
        return carry

    mine = pl.ds(pl.multiple_of(core * H, H), H)
    other = pl.ds(pl.multiple_of((1 - core) * H, H), H)
    factor = 0.5 / math.sqrt(ROWS * COLS * SLOTS)

    def probe_sum(ms):
        copy = go(pg.at[ms, :, other], half.at[ms], partner)
        yield
        copy.wait_recv()
        half[ms] += pg[ms, :, mine]
        start = 0
        for peers, at, buf, size in ((line_a, a, rb1, H), (line_b, b, rb2, H // 4), (line_y, y, rb3, 8)):
            sent = []
            for d in range(1, 4):
                piece = pl.ds(pl.multiple_of(start + (at + d) % 4 * size, 8), size)
                sent.append(go(half.at[ms, piece], buf.at[d - 1, ms], peers[d - 1]))
            yield
            start = start + at * size
            for copy in sent:
                copy.wait_recv()
            half[ms, pl.ds(pl.multiple_of(start, 8), size)] += buf[0, ms] + buf[1, ms] + buf[2, ms]
        part, base = a // 2, a % 2 * H
        base = base + b * (H // 4)
        piece = pl.ds(pl.multiple_of(base + y * 8, 8), 8)
        newp[part, ms, piece, mine] = probe[part, ms, piece, mine] - factor * half[ms, pl.ds(pl.multiple_of(start, 8), 8)]
        for peers, at, size in ((line_y, base + y * 8, 8), (line_b, base, H // 4), (line_a, a % 2 * H, H)):
            ref = newp.at[part, ms, pl.ds(pl.multiple_of(at, 8), size), mine]
            sent = [go(ref, ref, p) for p in peers]
            yield
            for copy in sent:
                copy.wait_recv()
        ref = newp.at[:, ms, :, mine]
        copy = go(ref, ref, partner)
        yield
        copy.wait_recv()

    pg[...] = jnp.zeros_like(pg)
    chains = []

    def begin(ms):
        chains.append(probe_sum(ms))
        next(chains[-1])

    def turn():
        for chain in chains:
            next(chain, None)

    def two_pairs(q, carry):
        p = 2 * q
        back(p + 1, spec_b)
        collect(p, spec_a)
        back(p + 2, spec_a)
        collect(p + 1, spec_b)
        return carry

    back(0, spec_a)
    lax.fori_loop(0, PAIRS, two_pairs, 0)
    begin(slice(0, 2))
    lax.fori_loop(PAIRS, PAIRS + 1, two_pairs, 0)
    turn()
    back(3 * PAIRS - 1, spec_b)
    collect(3 * PAIRS - 2, spec_a)
    collect(3 * PAIRS - 1, spec_b)
    begin(slice(2, 3))
    turn()
    lax.fori_loop(0, SLOTS, settle, 0)

    def deposit(lo, hi):
        def block(q, carry):
            for k in range(2):
                total = [0.0] * 8
                for s in range(SLOTS):
                    at = geo[s * GEO + PLACES + q]
                    total = [total[j] + tall[s, k, at + j] for j in range(8)]
                pad[k, pl.ds(q * 8, 8)] = jnp.stack(total)
            return carry

        lax.fori_loop(lo // 8, hi // 8, block, 0)

    from_east, from_west = [], []

    def to_cols(lo, hi):
        from_east.append(go(pad.at[:, HT + lo : HT + hi, :, 0:H], from_cols.at[0, :, lo:hi], west))
        from_west.append(go(pad.at[:, HT + lo : HT + hi, :, H + N :], from_cols.at[1, :, lo:hi], east))

    deposit(0, HT)
    deposit(HT + TT, PT)
    from_below = go(pad.at[:, 0:HT], from_rows.at[0], up)
    from_above = go(pad.at[:, HT + TT :], from_rows.at[1], down)
    turn()
    deposit(2 * HT, TT)
    to_cols(HT, HT + 24)
    deposit(HT, 2 * HT)
    deposit(TT, TT + HT)
    turn()
    to_cols(HT + 24, HT + 48)
    from_below.wait_recv()
    pad[:, TT : TT + HT] += from_rows[0] * (r < ROWS - 1).astype(F32)
    from_above.wait_recv()
    pad[:, HT : 2 * HT] += from_rows[1] * (r > 0).astype(F32)
    turn()
    to_cols(HT + 48, HT + 72)
    turn()
    to_cols(HT + 72, TT - HT)
    to_cols(0, HT)
    to_cols(TT - HT, TT)
    again.wait()
    out[...] -= 0.25 * pad[:, HT : HT + TT, :, H : H + N].reshape(SLOTS, N, N)
    for _ in range(8):
        turn()
    for copy in from_east:
        copy.wait_recv()
    out[:, :, H:N] -= (from_cols[0] * ((c < COLS - 1).astype(F32) * 0.25)).reshape(SLOTS, N, H)
    for copy in from_west:
        copy.wait_recv()
    out[:, :, 0:H] -= (from_cols[1] * ((c > 0).astype(F32) * 0.25)).reshape(SLOTS, N, H)
    for copy in copies_out:
        copy.wait_send()


def on_device(object_field, probe_modes, amplitudes, scan_offsets, slot_counts):
    hbm = pl.BlockSpec(memory_space=pl.ANY)
    sm = pl.BlockSpec(memory_space=pltpu.SMEM)
    vm = pl.BlockSpec(memory_space=pltpu.VMEM)
    new_object, new_probe = pl.pallas_call(
        body,
        out_shape=(
            jax.ShapeDtypeStruct((SLOTS, N, N), F32),
            jax.ShapeDtypeStruct((2, MODES, N, N), F32),
        ),
        in_specs=[sm, sm, hbm, hbm, hbm, hbm, hbm, hbm],
        out_specs=(vm, vm),
        scratch_shapes=[
            pltpu.VMEM((2, PT, 8, 2 * N), F32),
            pltpu.VMEM((2, MODES, N, N), F32),
            pltpu.VMEM((8, N, N), BF16),
            pltpu.VMEM((N, N), BF16),
            pltpu.VMEM((2, N, H), F32),
            pltpu.VMEM((MODES, 2, N, N), F32),
            pltpu.VMEM((MODES, 2, N, N), F32),
            pltpu.VMEM((2, 2, MODES * N, N), BF16),
            pltpu.VMEM((2, 2, MODES * N, N), BF16),
            pltpu.VMEM((SLOTS * MODES * 2, N, N), BF16),
            pltpu.VMEM((SLOTS * MODES * 2, N, N), BF16),
            pltpu.VMEM((SLOTS, 2, N, N), F32),
            pltpu.VMEM((SLOTS, 2, TALL, 8, 2 * N), F32),
            pltpu.VMEM((2, 2, HT, 8, 2 * N), F32),
            pltpu.VMEM((2, 2, TT, 8, H), F32),
            pltpu.VMEM((MODES, 2 * N, N), F32),
            pltpu.VMEM((MODES, 2 * N, H), F32),
            pltpu.VMEM((3, MODES, H, H), F32),
            pltpu.VMEM((3, MODES, H // 4, H), F32),
            pltpu.VMEM((3, MODES, 8, H), F32),
            pltpu.SemaphoreType.DMA((6,)),
            pltpu.SemaphoreType.DMA((2, 12 + 14 + 20 * 2)),
        ],
        compiler_params=pltpu.CompilerParams(
            collective_id=1, has_side_effects=True, vmem_limit_bytes=60 * 2**20
        ),
        name="step",
    )(
        geometry(scan_offsets),
        slot_counts,
        object_field.reshape(2, TT, 8, N),
        object_field.reshape(SLOTS, N, N),
        probe_modes,
        amplitudes.reshape(SLOTS, N, N),
        jnp.asarray(tables()),
        jnp.asarray(spread_table()),
    )
    return new_object.reshape(object_field.shape), new_probe


def solution(mesh):
    placed = (
        P(None, "row", "col"),
        P(),
        P("row", "col", None, None, None),
        P("row", "col", None, None),
        P("row", "col"),
    )
    return jax.shard_map(
        on_device,
        mesh=mesh,
        in_specs=placed,
        out_specs=(P(None, "row", "col"), P()),
        check_vma=False,
    )
```

```python
import math

import jax
import jax.numpy as jnp
import ml_dtypes
import numpy as np
from jax import lax
from jax.experimental import pallas as pl
from jax.experimental.pallas import tpu as pltpu
from jax.sharding import PartitionSpec as P

N = 256
H = 128
MODES = 3
PAD_R = 1280
T = 1024
SLOTS = 8
ROWS, COLS = 8, 16
MESH = pl.DeviceIdType.MESH
F32 = jnp.float32
BF16 = jnp.bfloat16
OBJ_R = 8192
OBJ_C = 4096


def tables():
    n = np.arange(H)[:, None]
    k = np.arange(H)[None, :]
    out = []
    for odd in (0, 1):
        angle = 2.0 * np.pi * ((n * (2 * k + odd)) % N) / N
        c, s = np.cos(angle) / 16.0, np.sin(angle) / 16.0
        full = np.block([[c, -s], [s, c]])
        for matrix in (full, full.T):
            high = matrix.astype(ml_dtypes.bfloat16)
            low = (matrix - high.astype(np.float64)).astype(ml_dtypes.bfloat16)
            out += [high, low]
    return np.stack(out)


def spread_table():
    matrix = np.zeros((N, N), np.float32)
    matrix[np.arange(0, N, 2), np.arange(H)] = 1.0
    matrix[np.arange(1, N, 2), np.arange(H) + H] = 1.0
    return matrix.astype(ml_dtypes.bfloat16)


def split(x):
    high = x.astype(BF16)
    return high, (x - high.astype(F32)).astype(BF16)


def right(pair, high, low):
    xh, xl = pair
    return jnp.dot(
        jnp.concatenate([xh, xl, xh], axis=1), jnp.concatenate([high, high, low], axis=0), preferred_element_type=F32
    )


def left(high, low, pair):
    xh, xl = pair
    return jnp.dot(
        jnp.concatenate([high, low, high], axis=1), jnp.concatenate([xh, xh, xl], axis=0), preferred_element_type=F32
    )


def beside(a, b):
    return jnp.concatenate([a, b], axis=1)


def above(a, b):
    return jnp.concatenate([a, b], axis=0)


def rows_up(tiles, shift, back, row8):
    t = [pltpu.roll(v, back, 0) for v in tiles]
    return jnp.concatenate([jnp.where(row8 < 8 - shift, p, q) for p, q in zip(t[:-1], t[1:])], axis=0)


def rows_down(v, shift, row8):
    t = pltpu.roll(v.reshape(N // 8, 8, N), shift, 1)
    none = jnp.zeros((1, 8, N), F32)
    return jnp.where(row8[None] >= shift, jnp.concatenate([t, none], axis=0), jnp.concatenate([none, t], axis=0))


GEO = 32
FIRST, SHIFT, LEFT, BACK_ROW, BACK_COL, ROW, PLACES = range(7)
HT, TT, PT = H // 8, T // 8, PAD_R // 8
EDGE = 8
TALL = 2 * EDGE + N // 8 + 1


def geometry(scan_offsets):
    off = scan_offsets.reshape(SLOTS, 2)
    top, lft = (off[:, 0] + H) % T, (off[:, 1] + H) % N
    shift = top % 8
    first = top // 8
    places = jnp.clip(jnp.arange(0, PT, 8)[None] - first[:, None] + EDGE, 0, TALL - 8)
    fixed = jnp.stack([first, shift, lft, (8 - shift) % 8, (N - lft) % N, off[:, 0]], axis=1)
    table = jnp.concatenate([fixed, places], axis=1).astype(jnp.int32)
    return jnp.pad(table, ((0, 0), (0, GEO - table.shape[1]))).reshape(SLOTS * GEO)


def body(
    geo, cnt, obj, obj_flat, probe_hbm, amp_hbm, tab_hbm, spread_hbm,
    out, newp,
    pad, probe, tab, spread, halves, spec_a, spec_b, wave_a, wave_b, sh, sl, patch, tall, from_rows, from_cols,
    pg, half, rb1, rb2, rb3, local, sems,
):
    r, c = lax.axis_index("row"), lax.axis_index("col")
    up, down = ((r + ROWS - 1) % ROWS, c), ((r + 1) % ROWS, c)
    west, east = (r, (c + COLS - 1) % COLS), (r, (c + 1) % COLS)
    x, core, z, y = r // 2, r % 2, c // 4, c % 4
    partner = (x * 2 + 1 - core, c)
    a, b = x, z

    def dev(a_, b_, y_):
        return (a_ * 2 + core, b_ * 4 + y_)

    line_a = [dev((a + d) % 4, b, y) for d in range(1, 4)]
    line_b = [dev(a, (b + d) % 4, y) for d in range(1, 4)]
    line_y = [dev(a, b, (y + d) % 4) for d in range(1, 4)]

    fetch = [
        pltpu.make_async_copy(src, dst, local.at[i])
        for i, (src, dst) in enumerate(
            (
                (obj, pad.at[:, HT : HT + TT, :, H : H + N]),
                (amp_hbm, out),
                (spread_hbm, spread),
                (probe_hbm, probe),
                (tab_hbm, tab),
            )
        )
    ]
    for f in fetch:
        f.start()

    peers = line_a + line_b + line_y + [up, down, west, east]
    barrier = pltpu.get_barrier_semaphore()
    for p in peers:
        pl.semaphore_signal(barrier, inc=1, device_id=p, device_id_type=MESH)
    pl.semaphore_wait(barrier, len(peers))

    count, copies_out = [0], []

    def go(src, dst, where):
        i = count[0]
        count[0] += 1
        copy = pltpu.make_async_remote_copy(
            src_ref=src, dst_ref=dst, send_sem=sems.at[0, i], recv_sem=sems.at[1, i], device_id=where, device_id_type=MESH
        )
        copy.start()
        copies_out.append(copy)
        return copy

    cols = []
    for lo, hi in ((0, HT), (TT - HT, TT), (HT, TT - HT)):
        cols.append(go(obj.at[:, lo:hi, :, H:N], pad.at[:, HT + lo : HT + hi, :, 0:H], east))
        cols.append(go(obj.at[:, lo:hi, :, 0:H], pad.at[:, HT + lo : HT + hi, :, H + N :], west))
    rows = [
        go(obj.at[:, TT - HT : TT], pad.at[:, 0:HT, :, H : H + N], down),
        go(obj.at[:, 0:HT], pad.at[:, HT + TT :, :, H : H + N], up),
    ]
    for k, lanes in ((0, slice(0, H)), (1, slice(H + N, 2 * N))):
        cols[k].wait_recv()
        rows.append(go(pad.at[:, HT : 2 * HT, :, lanes], pad.at[:, HT + TT :, :, lanes], up))
        cols[2 + k].wait_recv()
        rows.append(go(pad.at[:, TT : TT + HT, :, lanes], pad.at[:, 0:HT, :, lanes], down))

    fetch[1].wait()
    fetch[2].wait()

    def order(s, carry):
        halves[0] = out[s, :, 0:H]
        halves[1] = out[s, :, H:N]
        v = above(*(beside(*(halves[i, pl.ds(o, H, 2), :] for i in range(2))) for o in range(2)))
        vh, vl = split(v)
        out[s] = jnp.dot(beside(vh, vl), above(spread[...], spread[...]), preferred_element_type=F32)
        tall[s] = jnp.zeros((2, TALL, 8, 2 * N), F32)
        return carry

    lax.fori_loop(0, SLOTS, order, 0)
    for f in (fetch[0], fetch[3], fetch[4]):
        f.wait()
    for copy in rows + cols[4:]:
        copy.wait_recv()
    for copy in rows + cols:
        copy.wait_send()
    del copies_out[:]

    lane = lax.broadcasted_iota(jnp.int32, (N, N), 1)
    sub = lax.broadcasted_iota(jnp.int32, (N, N), 0)
    row8 = lax.broadcasted_iota(jnp.int32, (8, N), 0)
    lane33 = lax.broadcasted_iota(jnp.int32, (N // 8 + 1, 8, N), 2)
    col0 = c * N - H

    def window(s, wave):
        g = s * GEO
        first, shift, lft = geo[g + FIRST], geo[g + SHIFT], geo[g + LEFT]
        row = sub + geo[g + ROW]
        row_ok = (row >= 0) & (row < OBJ_R)
        ok_first = row_ok & (lane >= lft) & (lane + col0 >= 0)
        ok_second = row_ok & (lane < lft) & (lane + (col0 + N) < OBJ_C)
        parts = []
        for i in range(2):
            sides = []
            for lanes in (slice(0, N), slice(N, 2 * N)):
                tiles = [pad[i, first + k, :, lanes] for k in range(N // 8 + 1)]
                sides.append(rows_up(tiles, shift, geo[g + BACK_ROW], row8))
            v = jnp.where(ok_first, sides[0], jnp.where(ok_second, sides[1], 0.0))
            parts.append(pltpu.roll(v, geo[g + BACK_COL], 1))
        pr, pi = parts
        patch[s, 0] = pr
        patch[s, 1] = pi
        for m in range(MODES):
            qr, qi = probe[0, m], probe[1, m]
            wr = qr * pr - qi * pi
            wi = qr * pi + qi * pr
            rows = slice(m * N, (m + 1) * N)
            plus = beside(wr[:, :H] + wr[:, H:], wi[:, :H] + wi[:, H:])
            wave[0, 0, rows], wave[0, 1, rows] = split(plus)
            minus = beside(wr[:, :H] - wr[:, H:], wi[:, :H] - wi[:, H:])
            wave[1, 0, rows], wave[1, 1, rows] = split(minus)

    def transform(wave, spec):
        ye = right((wave[0, 0], wave[0, 1]), tab[0], tab[1])
        yo = right((wave[1, 0], wave[1, 1]), tab[4], tab[5])
        for m in range(MODES):
            k = m * N
            for i, sign in enumerate((1.0, -1.0)):
                e = ye[k : k + H] + sign * ye[k + H : k + N]
                o = yo[k : k + H] + sign * yo[k + H : k + N]
                part = above(beside(e[:, :H], o[:, :H]), beside(e[:, H:], o[:, H:]))
                spec[m, i] = left(tab[2 + 4 * i], tab[3 + 4 * i], split(part))

    def scale(s, spec):
        live = jnp.where(s < cnt[0, 0], 1.0, 0.0)
        for i in range(2):
            power = 0.0
            for m in range(MODES):
                v = spec[m, i]
                power = power + (v[:H] * v[:H] + v[H:] * v[H:])
            ratio = live * (1.0 - out[s, i * H : (i + 1) * H] * lax.rsqrt(jnp.maximum(power, 1.0)))
            ratio = above(ratio, ratio)
            for m in range(MODES):
                k = (s * MODES + m) * 2 + i
                sh[k], sl[k] = split(spec[m, i] * ratio)

    def two_slots(q, carry):
        s = 2 * q
        transform(wave_a, spec_a)
        window(s + 1, wave_b)
        scale((s + SLOTS - 1) % SLOTS, spec_b)
        transform(wave_b, spec_b)
        window((s + 2) % SLOTS, wave_a)
        scale(s, spec_a)
        return carry

    spec_b[...] = jnp.zeros_like(spec_b)
    window(0, wave_a)
    lax.fori_loop(0, SLOTS // 2, two_slots, 0)
    scale(SLOTS - 1, spec_b)
    again = pltpu.make_async_copy(obj_flat, out, local.at[5])
    again.start()

    PAIRS = SLOTS // 2

    def back(p, spec):
        m, j = p // PAIRS, p % PAIRS
        even, odd = [], []
        for t in range(2):
            k = ((2 * j + t) * MODES + m) * 2
            e = left(tab[0], tab[1], (sh[k], sl[k]))
            o = left(tab[4], tab[5], (sh[k + 1], sl[k + 1]))
            lo, hi = e + o, e - o
            even += [beside(lo[:H, :H], lo[H:, :H]), beside(hi[:H, :H], hi[H:, :H])]
            odd += [beside(lo[:H, H:], lo[H:, H:]), beside(hi[:H, H:], hi[H:, H:])]
        e = right(split(jnp.concatenate(even, axis=0)), tab[2], tab[3])
        o = right(split(jnp.concatenate(odd, axis=0)), tab[6], tab[7])
        for t in range(2):
            spec[t, 0] = e[t * N : (t + 1) * N]
            spec[t, 1] = o[t * N : (t + 1) * N]

    inner = slice(EDGE, EDGE + N // 8)

    def collect(p, spec):
        m, j = p // PAIRS, p % PAIRS
        mode_r, mode_i = 0.0, 0.0
        qr, qi = probe[0, m], probe[1, m]
        for t in range(2):
            s = 2 * j + t
            ee, oo = spec[t, 0], spec[t, 1]
            lo, hi = ee + oo, ee - oo
            cr = beside(lo[:, :H], hi[:, :H])
            ci = beside(lo[:, H:], hi[:, H:])
            pr, pi = patch[s, 0], patch[s, 1]
            mode_r = mode_r + (pr * cr + pi * ci)
            mode_i = mode_i + (pr * ci - pi * cr)
            for k, g in enumerate((qr * cr + qi * ci, qr * ci - qi * cr)):
                tall[s, k, inner, :, 0:N] += g.reshape(N // 8, 8, N)
        pg[m, 0:N] += mode_r
        pg[m, N:] += mode_i

    def settle(s, carry):
        lft = geo[s * GEO + LEFT]
        for k in range(2):
            g = pltpu.roll(tall[s, k, inner, :, 0:N].reshape(N, N), lft, 1)
            g = rows_down(g, geo[s * GEO + SHIFT], row8)
            first = jnp.where(lane33 >= lft, g, 0.0)
            tall[s, k, EDGE : TALL - EDGE, :, 0:N] = first
            tall[s, k, EDGE : TALL - EDGE, :, N : 2 * N] = g - first
        return carry

    mine = pl.ds(pl.multiple_of(core * H, H), H)
    other = pl.ds(pl.multiple_of((1 - core) * H, H), H)
    factor = 0.5 / math.sqrt(ROWS * COLS * SLOTS)

    def probe_sum(ms):
        copy = go(pg.at[ms, :, other], half.at[ms], partner)
        yield
        copy.wait_recv()
        half[ms] += pg[ms, :, mine]
        start = 0
        for peers, at, buf, size in ((line_b, b, rb1, H), (line_a, a, rb2, H // 4), (line_y, y, rb3, 8)):
            sent = []
            for d in range(1, 4):
                piece = pl.ds(pl.multiple_of(start + (at + d) % 4 * size, 8), size)
                sent.append(go(half.at[ms, piece], buf.at[d - 1, ms], peers[d - 1]))
            yield
            start = start + at * size
            for copy in sent:
                copy.wait_recv()
            half[ms, pl.ds(pl.multiple_of(start, 8), size)] += buf[0, ms] + buf[1, ms] + buf[2, ms]
        part, base = b // 2, b % 2 * H + a * (H // 4)
        piece = pl.ds(pl.multiple_of(base + y * 8, 8), 8)
        newp[part, ms, piece, mine] = probe[part, ms, piece, mine] - factor * half[ms, pl.ds(pl.multiple_of(start, 8), 8)]
        for peers, at, size in ((line_y, base + y * 8, 8), (line_b, base, H // 4)):
            ref = newp.at[part, ms, pl.ds(pl.multiple_of(at, 8), size), mine]
            sent = [go(ref, ref, p) for p in peers]
            yield
            for copy in sent:
                copy.wait_recv()
        sent = []
        for low in range(0, N, H):
            ref = newp.at[:, ms, pl.ds(pl.multiple_of(low + a * (H // 4), 8), H // 4), mine]
            sent += [go(ref, ref, p) for p in line_a]
        yield
        for copy in sent:
            copy.wait_recv()
        ref = newp.at[:, ms, :, mine]
        copy = go(ref, ref, partner)
        yield
        copy.wait_recv()

    pg[...] = jnp.zeros_like(pg)
    chains = []

    def begin(ms):
        chains.append(probe_sum(ms))
        next(chains[-1])

    def turn():
        for chain in chains:
            next(chain, None)

    def two_pairs(q, carry):
        p = 2 * q
        back(p + 1, spec_b)
        collect(p, spec_a)
        back(p + 2, spec_a)
        collect(p + 1, spec_b)
        return carry

    back(0, spec_a)
    lax.fori_loop(0, PAIRS, two_pairs, 0)
    begin(slice(0, 2))
    lax.fori_loop(PAIRS, PAIRS + 1, two_pairs, 0)
    turn()
    back(3 * PAIRS - 1, spec_b)
    collect(3 * PAIRS - 2, spec_a)
    collect(3 * PAIRS - 1, spec_b)
    begin(slice(2, 3))
    turn()
    lax.fori_loop(0, SLOTS, settle, 0)

    def deposit(lo, hi):
        def block(q, carry):
            for k in range(2):
                total = [0.0] * 8
                for s in range(SLOTS):
                    at = geo[s * GEO + PLACES + q]
                    total = [total[j] + tall[s, k, at + j] for j in range(8)]
                pad[k, pl.ds(q * 8, 8)] = jnp.stack(total)
            return carry

        lax.fori_loop(lo // 8, hi // 8, block, 0)

    from_east, from_west = [], []

    def to_cols(lo, hi):
        from_east.append(go(pad.at[:, HT + lo : HT + hi, :, 0:H], from_cols.at[0, :, lo:hi], west))
        from_west.append(go(pad.at[:, HT + lo : HT + hi, :, H + N :], from_cols.at[1, :, lo:hi], east))

    deposit(0, HT)
    deposit(HT + TT, PT)
    from_below = go(pad.at[:, 0:HT], from_rows.at[0], up)
    from_above = go(pad.at[:, HT + TT :], from_rows.at[1], down)
    turn()
    deposit(2 * HT, TT)
    to_cols(HT, HT + 24)
    deposit(HT, 2 * HT)
    deposit(TT, TT + HT)
    turn()
    to_cols(HT + 24, HT + 48)
    from_below.wait_recv()
    pad[:, TT : TT + HT] += from_rows[0] * (r < ROWS - 1).astype(F32)
    from_above.wait_recv()
    pad[:, HT : 2 * HT] += from_rows[1] * (r > 0).astype(F32)
    turn()
    to_cols(HT + 48, HT + 72)
    turn()
    to_cols(HT + 72, TT - HT)
    to_cols(0, HT)
    to_cols(TT - HT, TT)
    again.wait()
    out[...] -= 0.25 * pad[:, HT : HT + TT, :, H : H + N].reshape(SLOTS, N, N)
    for _ in range(8):
        turn()
    for copy in from_east:
        copy.wait_recv()
    out[:, :, H:N] -= (from_cols[0] * ((c < COLS - 1).astype(F32) * 0.25)).reshape(SLOTS, N, H)
    for copy in from_west:
        copy.wait_recv()
    out[:, :, 0:H] -= (from_cols[1] * ((c > 0).astype(F32) * 0.25)).reshape(SLOTS, N, H)
    for copy in copies_out:
        copy.wait_send()


def on_device(object_field, probe_modes, amplitudes, scan_offsets, slot_counts):
    hbm = pl.BlockSpec(memory_space=pl.ANY)
    sm = pl.BlockSpec(memory_space=pltpu.SMEM)
    vm = pl.BlockSpec(memory_space=pltpu.VMEM)
    new_object, new_probe = pl.pallas_call(
        body,
        out_shape=(
            jax.ShapeDtypeStruct((SLOTS, N, N), F32),
            jax.ShapeDtypeStruct((2, MODES, N, N), F32),
        ),
        in_specs=[sm, sm, hbm, hbm, hbm, hbm, hbm, hbm],
        out_specs=(vm, vm),
        scratch_shapes=[
            pltpu.VMEM((2, PT, 8, 2 * N), F32),
            pltpu.VMEM((2, MODES, N, N), F32),
            pltpu.VMEM((8, N, N), BF16),
            pltpu.VMEM((N, N), BF16),
            pltpu.VMEM((2, N, H), F32),
            pltpu.VMEM((MODES, 2, N, N), F32),
            pltpu.VMEM((MODES, 2, N, N), F32),
            pltpu.VMEM((2, 2, MODES * N, N), BF16),
            pltpu.VMEM((2, 2, MODES * N, N), BF16),
            pltpu.VMEM((SLOTS * MODES * 2, N, N), BF16),
            pltpu.VMEM((SLOTS * MODES * 2, N, N), BF16),
            pltpu.VMEM((SLOTS, 2, N, N), F32),
            pltpu.VMEM((SLOTS, 2, TALL, 8, 2 * N), F32),
            pltpu.VMEM((2, 2, HT, 8, 2 * N), F32),
            pltpu.VMEM((2, 2, TT, 8, H), F32),
            pltpu.VMEM((MODES, 2 * N, N), F32),
            pltpu.VMEM((MODES, 2 * N, H), F32),
            pltpu.VMEM((3, MODES, H, H), F32),
            pltpu.VMEM((3, MODES, H // 4, H), F32),
            pltpu.VMEM((3, MODES, 8, H), F32),
            pltpu.SemaphoreType.DMA((6,)),
            pltpu.SemaphoreType.DMA((2, 12 + 14 + 23 * 2)),
        ],
        compiler_params=pltpu.CompilerParams(
            collective_id=1, has_side_effects=True, vmem_limit_bytes=60 * 2**20
        ),
        name="step",
    )(
        geometry(scan_offsets),
        slot_counts,
        object_field.reshape(2, TT, 8, N),
        object_field.reshape(SLOTS, N, N),
        probe_modes,
        amplitudes.reshape(SLOTS, N, N),
        jnp.asarray(tables()),
        jnp.asarray(spread_table()),
    )
    return new_object.reshape(object_field.shape), new_probe


def solution(mesh):
    placed = (
        P(None, "row", "col"),
        P(),
        P("row", "col", None, None, None),
        P("row", "col", None, None),
        P("row", "col"),
    )
    return jax.shard_map(
        on_device,
        mesh=mesh,
        in_specs=placed,
        out_specs=(P(None, "row", "col"), P()),
        check_vma=False,
    )
```

```python
import math

import jax
import jax.numpy as jnp
import ml_dtypes
import numpy as np
from jax import lax
from jax.experimental import pallas as pl
from jax.experimental.pallas import tpu as pltpu
from jax.sharding import PartitionSpec as P

N = 256
H = 128
MODES = 3
PAD_R = 1280
T = 1024
SLOTS = 8
ROWS, COLS = 8, 16
MESH = pl.DeviceIdType.MESH
F32 = jnp.float32
BF16 = jnp.bfloat16
OBJ_R = 8192
OBJ_C = 4096


def tables():
    n = np.arange(H)[:, None]
    k = np.arange(H)[None, :]
    out = []
    for odd in (0, 1):
        angle = 2.0 * np.pi * ((n * (2 * k + odd)) % N) / N
        c, s = np.cos(angle) / 16.0, np.sin(angle) / 16.0
        full = np.block([[c, -s], [s, c]])
        for matrix in (full, full.T):
            high = matrix.astype(ml_dtypes.bfloat16)
            low = (matrix - high.astype(np.float64)).astype(ml_dtypes.bfloat16)
            out += [high, low]
    return np.stack(out)


def spread_table():
    matrix = np.zeros((N, N), np.float32)
    matrix[np.arange(0, N, 2), np.arange(H)] = 1.0
    matrix[np.arange(1, N, 2), np.arange(H) + H] = 1.0
    return matrix.astype(ml_dtypes.bfloat16)


def split(x):
    high = x.astype(BF16)
    return high, (x - high.astype(F32)).astype(BF16)


def right(pair, high, low):
    xh, xl = pair
    return jnp.dot(
        jnp.concatenate([xh, xl, xh], axis=1), jnp.concatenate([high, high, low], axis=0), preferred_element_type=F32
    )


def left(high, low, pair):
    xh, xl = pair
    return jnp.dot(
        jnp.concatenate([high, low, high], axis=1), jnp.concatenate([xh, xh, xl], axis=0), preferred_element_type=F32
    )


def beside(a, b):
    return jnp.concatenate([a, b], axis=1)


def above(a, b):
    return jnp.concatenate([a, b], axis=0)


def rows_up(tiles, shift, back, row8):
    t = [pltpu.roll(v, back, 0) for v in tiles]
    return jnp.concatenate([jnp.where(row8 < 8 - shift, p, q) for p, q in zip(t[:-1], t[1:])], axis=0)


def rows_down(v, shift, row8):
    t = pltpu.roll(v.reshape(N // 8, 8, N), shift, 1)
    none = jnp.zeros((1, 8, N), F32)
    return jnp.where(row8[None] >= shift, jnp.concatenate([t, none], axis=0), jnp.concatenate([none, t], axis=0))


GEO = 32
FIRST, SHIFT, LEFT, BACK_ROW, BACK_COL, ROW, PLACES = range(7)
HT, TT, PT = H // 8, T // 8, PAD_R // 8
EDGE = 8
TALL = 2 * EDGE + N // 8 + 1


def geometry(scan_offsets):
    off = scan_offsets.reshape(SLOTS, 2)
    top, lft = (off[:, 0] + H) % T, (off[:, 1] + H) % N
    shift = top % 8
    first = top // 8
    places = jnp.clip(jnp.arange(0, PT, 8)[None] - first[:, None] + EDGE, 0, TALL - 8)
    fixed = jnp.stack([first, shift, lft, (8 - shift) % 8, (N - lft) % N, off[:, 0]], axis=1)
    table = jnp.concatenate([fixed, places], axis=1).astype(jnp.int32)
    return jnp.pad(table, ((0, 0), (0, GEO - table.shape[1]))).reshape(SLOTS * GEO)


def body(
    geo, cnt, obj, obj_flat, probe_hbm, amp_hbm, tab_hbm, spread_hbm,
    out, newp,
    pad, probe, tab, spread, halves, spec_a, spec_b, wave_a, wave_b, sh, sl, patch, tall, from_rows, from_cols,
    pg, half, rb1, rb2, rb3, local, sems,
):
    r, c = lax.axis_index("row"), lax.axis_index("col")
    up, down = ((r + ROWS - 1) % ROWS, c), ((r + 1) % ROWS, c)
    west, east = (r, (c + COLS - 1) % COLS), (r, (c + 1) % COLS)
    x, core, z, y = r // 2, r % 2, c // 4, c % 4
    partner = (x * 2 + 1 - core, c)
    a, b = x + core * (z - x), z + core * (x - z)

    def dev(a_, b_, y_):
        return ((a_ + core * (b_ - a_)) * 2 + core, (b_ + core * (a_ - b_)) * 4 + y_)

    line_a = [dev((a + d) % 4, b, y) for d in range(1, 4)]
    line_b = [dev(a, (b + d) % 4, y) for d in range(1, 4)]
    line_y = [dev(a, b, (y + d) % 4) for d in range(1, 4)]

    fetch = [
        pltpu.make_async_copy(src, dst, local.at[i])
        for i, (src, dst) in enumerate(
            (
                (obj, pad.at[:, HT : HT + TT, :, H : H + N]),
                (amp_hbm, out),
                (spread_hbm, spread),
                (probe_hbm, probe),
                (tab_hbm, tab),
            )
        )
    ]
    for f in fetch:
        f.start()

    peers = line_a + line_b + line_y + [up, down, west, east]
    barrier = pltpu.get_barrier_semaphore()
    for p in peers:
        pl.semaphore_signal(barrier, inc=1, device_id=p, device_id_type=MESH)
    pl.semaphore_wait(barrier, len(peers))

    count, copies_out = [0], []

    def go(src, dst, where):
        i = count[0]
        count[0] += 1
        copy = pltpu.make_async_remote_copy(
            src_ref=src, dst_ref=dst, send_sem=sems.at[0, i], recv_sem=sems.at[1, i], device_id=where, device_id_type=MESH
        )
        copy.start()
        copies_out.append(copy)
        return copy

    cols = []
    for lo, hi in ((0, HT), (TT - HT, TT), (HT, TT - HT)):
        cols.append(go(obj.at[:, lo:hi, :, H:N], pad.at[:, HT + lo : HT + hi, :, 0:H], east))
        cols.append(go(obj.at[:, lo:hi, :, 0:H], pad.at[:, HT + lo : HT + hi, :, H + N :], west))
    rows = [
        go(obj.at[:, TT - HT : TT], pad.at[:, 0:HT, :, H : H + N], down),
        go(obj.at[:, 0:HT], pad.at[:, HT + TT :, :, H : H + N], up),
    ]
    for k, lanes in ((0, slice(0, H)), (1, slice(H + N, 2 * N))):
        cols[k].wait_recv()
        rows.append(go(pad.at[:, HT : 2 * HT, :, lanes], pad.at[:, HT + TT :, :, lanes], up))
        cols[2 + k].wait_recv()
        rows.append(go(pad.at[:, TT : TT + HT, :, lanes], pad.at[:, 0:HT, :, lanes], down))

    fetch[1].wait()
    fetch[2].wait()

    def order(s, carry):
        halves[0] = out[s, :, 0:H]
        halves[1] = out[s, :, H:N]
        v = above(*(beside(*(halves[i, pl.ds(o, H, 2), :] for i in range(2))) for o in range(2)))
        vh, vl = split(v)
        out[s] = jnp.dot(beside(vh, vl), above(spread[...], spread[...]), preferred_element_type=F32)
        tall[s] = jnp.zeros((2, TALL, 8, 2 * N), F32)
        return carry

    lax.fori_loop(0, SLOTS, order, 0)
    for f in (fetch[0], fetch[3], fetch[4]):
        f.wait()
    for copy in rows + cols[4:]:
        copy.wait_recv()
    for copy in rows + cols:
        copy.wait_send()
    del copies_out[:]

    lane = lax.broadcasted_iota(jnp.int32, (N, N), 1)
    sub = lax.broadcasted_iota(jnp.int32, (N, N), 0)
    row8 = lax.broadcasted_iota(jnp.int32, (8, N), 0)
    lane33 = lax.broadcasted_iota(jnp.int32, (N // 8 + 1, 8, N), 2)
    col0 = c * N - H

    def window(s, wave):
        g = s * GEO
        first, shift, lft = geo[g + FIRST], geo[g + SHIFT], geo[g + LEFT]
        row = sub + geo[g + ROW]
        row_ok = (row >= 0) & (row < OBJ_R)
        ok_first = row_ok & (lane >= lft) & (lane + col0 >= 0)
        ok_second = row_ok & (lane < lft) & (lane + (col0 + N) < OBJ_C)
        parts = []
        for i in range(2):
            sides = []
            for lanes in (slice(0, N), slice(N, 2 * N)):
                tiles = [pad[i, first + k, :, lanes] for k in range(N // 8 + 1)]
                sides.append(rows_up(tiles, shift, geo[g + BACK_ROW], row8))
            v = jnp.where(ok_first, sides[0], jnp.where(ok_second, sides[1], 0.0))
            parts.append(pltpu.roll(v, geo[g + BACK_COL], 1))
        pr, pi = parts
        patch[s, 0] = pr
        patch[s, 1] = pi
        for m in range(MODES):
            qr, qi = probe[0, m], probe[1, m]
            wr = qr * pr - qi * pi
            wi = qr * pi + qi * pr
            rows = slice(m * N, (m + 1) * N)
            plus = beside(wr[:, :H] + wr[:, H:], wi[:, :H] + wi[:, H:])
            wave[0, 0, rows], wave[0, 1, rows] = split(plus)
            minus = beside(wr[:, :H] - wr[:, H:], wi[:, :H] - wi[:, H:])
            wave[1, 0, rows], wave[1, 1, rows] = split(minus)

    def transform(wave, spec):
        ye = right((wave[0, 0], wave[0, 1]), tab[0], tab[1])
        yo = right((wave[1, 0], wave[1, 1]), tab[4], tab[5])
        for m in range(MODES):
            k = m * N
            for i, sign in enumerate((1.0, -1.0)):
                e = ye[k : k + H] + sign * ye[k + H : k + N]
                o = yo[k : k + H] + sign * yo[k + H : k + N]
                part = above(beside(e[:, :H], o[:, :H]), beside(e[:, H:], o[:, H:]))
                spec[m, i] = left(tab[2 + 4 * i], tab[3 + 4 * i], split(part))

    def scale(s, spec):
        live = jnp.where(s < cnt[0, 0], 1.0, 0.0)
        for i in range(2):
            power = 0.0
            for m in range(MODES):
                v = spec[m, i]
                power = power + (v[:H] * v[:H] + v[H:] * v[H:])
            ratio = live * (1.0 - out[s, i * H : (i + 1) * H] * lax.rsqrt(jnp.maximum(power, 1.0)))
            ratio = above(ratio, ratio)
            for m in range(MODES):
                k = (s * MODES + m) * 2 + i
                sh[k], sl[k] = split(spec[m, i] * ratio)

    def two_slots(q, carry):
        s = 2 * q
        transform(wave_a, spec_a)
        window(s + 1, wave_b)
        scale((s + SLOTS - 1) % SLOTS, spec_b)
        transform(wave_b, spec_b)
        window((s + 2) % SLOTS, wave_a)
        scale(s, spec_a)
        return carry

    spec_b[...] = jnp.zeros_like(spec_b)
    window(0, wave_a)
    lax.fori_loop(0, SLOTS // 2, two_slots, 0)
    scale(SLOTS - 1, spec_b)
    again = pltpu.make_async_copy(obj_flat, out, local.at[5])
    again.start()

    PAIRS = SLOTS // 2

    def back(p, spec):
        m, j = p // PAIRS, p % PAIRS
        even, odd = [], []
        for t in range(2):
            k = ((2 * j + t) * MODES + m) * 2
            e = left(tab[0], tab[1], (sh[k], sl[k]))
            o = left(tab[4], tab[5], (sh[k + 1], sl[k + 1]))
            lo, hi = e + o, e - o
            even += [beside(lo[:H, :H], lo[H:, :H]), beside(hi[:H, :H], hi[H:, :H])]
            odd += [beside(lo[:H, H:], lo[H:, H:]), beside(hi[:H, H:], hi[H:, H:])]
        e = right(split(jnp.concatenate(even, axis=0)), tab[2], tab[3])
        o = right(split(jnp.concatenate(odd, axis=0)), tab[6], tab[7])
        for t in range(2):
            spec[t, 0] = e[t * N : (t + 1) * N]
            spec[t, 1] = o[t * N : (t + 1) * N]

    inner = slice(EDGE, EDGE + N // 8)

    def collect(p, spec):
        m, j = p // PAIRS, p % PAIRS
        mode_r, mode_i = 0.0, 0.0
        qr, qi = probe[0, m], probe[1, m]
        for t in range(2):
            s = 2 * j + t
            ee, oo = spec[t, 0], spec[t, 1]
            lo, hi = ee + oo, ee - oo
            cr = beside(lo[:, :H], hi[:, :H])
            ci = beside(lo[:, H:], hi[:, H:])
            pr, pi = patch[s, 0], patch[s, 1]
            mode_r = mode_r + (pr * cr + pi * ci)
            mode_i = mode_i + (pr * ci - pi * cr)
            for k, g in enumerate((qr * cr + qi * ci, qr * ci - qi * cr)):
                tall[s, k, inner, :, 0:N] += g.reshape(N // 8, 8, N)
        pg[m, 0:N] += mode_r
        pg[m, N:] += mode_i

    def settle(s, carry):
        lft = geo[s * GEO + LEFT]
        for k in range(2):
            g = pltpu.roll(tall[s, k, inner, :, 0:N].reshape(N, N), lft, 1)
            g = rows_down(g, geo[s * GEO + SHIFT], row8)
            first = jnp.where(lane33 >= lft, g, 0.0)
            tall[s, k, EDGE : TALL - EDGE, :, 0:N] = first
            tall[s, k, EDGE : TALL - EDGE, :, N : 2 * N] = g - first
        return carry

    mine = pl.ds(pl.multiple_of(core * H, H), H)
    other = pl.ds(pl.multiple_of((1 - core) * H, H), H)
    factor = 0.5 / math.sqrt(ROWS * COLS * SLOTS)

    def probe_sum(ms):
        copy = go(pg.at[ms, :, other], half.at[ms], partner)
        yield
        copy.wait_recv()
        half[ms] += pg[ms, :, mine]
        start = 0
        for peers, at, buf, size in ((line_a, a, rb1, H), (line_b, b, rb2, H // 4), (line_y, y, rb3, 8)):
            sent = []
            for d in range(1, 4):
                piece = pl.ds(pl.multiple_of(start + (at + d) % 4 * size, 8), size)
                sent.append(go(half.at[ms, piece], buf.at[d - 1, ms], peers[d - 1]))
            yield
            start = start + at * size
            for copy in sent:
                copy.wait_recv()
            half[ms, pl.ds(pl.multiple_of(start, 8), size)] += buf[0, ms] + buf[1, ms] + buf[2, ms]
        part, base = a // 2, a % 2 * H
        base = base + b * (H // 4)
        piece = pl.ds(pl.multiple_of(base + y * 8, 8), 8)
        newp[part, ms, piece, mine] = probe[part, ms, piece, mine] - factor * half[ms, pl.ds(pl.multiple_of(start, 8), 8)]
        for peers, at, size in ((line_y, base + y * 8, 8), (line_b, base, H // 4), (line_a, a % 2 * H, H)):
            ref = newp.at[part, ms, pl.ds(pl.multiple_of(at, 8), size), mine]
            sent = [go(ref, ref, p) for p in peers]
            yield
            for copy in sent:
                copy.wait_recv()
        ref = newp.at[:, ms, :, mine]
        copy = go(ref, ref, partner)
        yield
        copy.wait_recv()

    pg[...] = jnp.zeros_like(pg)
    chains = []

    def begin(ms):
        chains.append(probe_sum(ms))
        next(chains[-1])

    def turn():
        for chain in chains:
            next(chain, None)

    def two_pairs(q, carry):
        p = 2 * q
        back(p + 1, spec_b)
        collect(p, spec_a)
        back(p + 2, spec_a)
        collect(p + 1, spec_b)
        return carry

    back(0, spec_a)
    lax.fori_loop(0, PAIRS, two_pairs, 0)
    begin(slice(0, 2))
    lax.fori_loop(PAIRS, PAIRS + 1, two_pairs, 0)
    turn()
    back(3 * PAIRS - 1, spec_b)
    collect(3 * PAIRS - 2, spec_a)
    collect(3 * PAIRS - 1, spec_b)
    begin(slice(2, 3))
    turn()
    lax.fori_loop(0, SLOTS, settle, 0)

    def deposit(lo, hi):
        def block(q, carry):
            for k in range(2):
                total = [0.0] * 8
                for s in range(SLOTS):
                    at = geo[s * GEO + PLACES + q]
                    total = [total[j] + tall[s, k, at + j] for j in range(8)]
                pad[k, pl.ds(q * 8, 8)] = jnp.stack(total)
            return carry

        lax.fori_loop(lo // 8, hi // 8, block, 0)

    from_east, from_west = [], []

    def to_cols(lo, hi):
        from_east.append(go(pad.at[:, HT + lo : HT + hi, :, 0:H], from_cols.at[0, :, lo:hi], west))
        from_west.append(go(pad.at[:, HT + lo : HT + hi, :, H + N :], from_cols.at[1, :, lo:hi], east))

    deposit(0, HT)
    deposit(HT + TT, PT)
    from_below = go(pad.at[:, 0:HT], from_rows.at[0], up)
    from_above = go(pad.at[:, HT + TT :], from_rows.at[1], down)
    turn()
    deposit(2 * HT, TT)
    to_cols(HT, HT + 24)
    deposit(HT, 2 * HT)
    deposit(TT, TT + HT)
    turn()
    to_cols(HT + 24, HT + 72)
    from_below.wait_recv()
    pad[:, TT : TT + HT] += from_rows[0] * (r < ROWS - 1).astype(F32)
    from_above.wait_recv()
    pad[:, HT : 2 * HT] += from_rows[1] * (r > 0).astype(F32)
    turn()
    to_cols(HT + 72, TT - HT)
    to_cols(0, HT)
    to_cols(TT - HT, TT)
    again.wait()
    out[...] -= 0.25 * pad[:, HT : HT + TT, :, H : H + N].reshape(SLOTS, N, N)
    for _ in range(8):
        turn()
    for copy in from_east:
        copy.wait_recv()
    out[:, :, H:N] -= (from_cols[0] * ((c < COLS - 1).astype(F32) * 0.25)).reshape(SLOTS, N, H)
    for copy in from_west:
        copy.wait_recv()
    out[:, :, 0:H] -= (from_cols[1] * ((c > 0).astype(F32) * 0.25)).reshape(SLOTS, N, H)
    for copy in copies_out:
        copy.wait_send()


def on_device(object_field, probe_modes, amplitudes, scan_offsets, slot_counts):
    hbm = pl.BlockSpec(memory_space=pl.ANY)
    sm = pl.BlockSpec(memory_space=pltpu.SMEM)
    vm = pl.BlockSpec(memory_space=pltpu.VMEM)
    new_object, new_probe = pl.pallas_call(
        body,
        out_shape=(
            jax.ShapeDtypeStruct((SLOTS, N, N), F32),
            jax.ShapeDtypeStruct((2, MODES, N, N), F32),
        ),
        in_specs=[sm, sm, hbm, hbm, hbm, hbm, hbm, hbm],
        out_specs=(vm, vm),
        scratch_shapes=[
            pltpu.VMEM((2, PT, 8, 2 * N), F32),
            pltpu.VMEM((2, MODES, N, N), F32),
            pltpu.VMEM((8, N, N), BF16),
            pltpu.VMEM((N, N), BF16),
            pltpu.VMEM((2, N, H), F32),
            pltpu.VMEM((MODES, 2, N, N), F32),
            pltpu.VMEM((MODES, 2, N, N), F32),
            pltpu.VMEM((2, 2, MODES * N, N), BF16),
            pltpu.VMEM((2, 2, MODES * N, N), BF16),
            pltpu.VMEM((SLOTS * MODES * 2, N, N), BF16),
            pltpu.VMEM((SLOTS * MODES * 2, N, N), BF16),
            pltpu.VMEM((SLOTS, 2, N, N), F32),
            pltpu.VMEM((SLOTS, 2, TALL, 8, 2 * N), F32),
            pltpu.VMEM((2, 2, HT, 8, 2 * N), F32),
            pltpu.VMEM((2, 2, TT, 8, H), F32),
            pltpu.VMEM((MODES, 2 * N, N), F32),
            pltpu.VMEM((MODES, 2 * N, H), F32),
            pltpu.VMEM((3, MODES, H, H), F32),
            pltpu.VMEM((3, MODES, H // 4, H), F32),
            pltpu.VMEM((3, MODES, 8, H), F32),
            pltpu.SemaphoreType.DMA((6,)),
            pltpu.SemaphoreType.DMA((2, 12 + 12 + 20 * 2)),
        ],
        compiler_params=pltpu.CompilerParams(
            collective_id=1, has_side_effects=True, vmem_limit_bytes=60 * 2**20
        ),
        name="step",
    )(
        geometry(scan_offsets),
        slot_counts,
        object_field.reshape(2, TT, 8, N),
        object_field.reshape(SLOTS, N, N),
        probe_modes,
        amplitudes.reshape(SLOTS, N, N),
        jnp.asarray(tables()),
        jnp.asarray(spread_table()),
    )
    return new_object.reshape(object_field.shape), new_probe


def solution(mesh):
    placed = (
        P(None, "row", "col"),
        P(),
        P("row", "col", None, None, None),
        P("row", "col", None, None),
        P("row", "col"),
    )
    return jax.shard_map(
        on_device,
        mesh=mesh,
        in_specs=placed,
        out_specs=(P(None, "row", "col"), P()),
        check_vma=False,
    )
```
